128 devices in a mesh: ny: 8 (over x, core), nx: 16 (over y, z).
Axes of the slice: x: 4, y: 4, z: 4, core: 2. Of those that a mesh axis runs over, the one named last changes fastest.
Arguments:
- elevation: float32 [1152, 18432], P('ny', 'nx'), may hold values from -6 to 6
- flux_x: float32 [1152, 18432], P('ny', 'nx'), may hold values from -3 to 3
- flux_y: float32 [1152, 18432], P('ny', 'nx'), may hold values from -3 to 3
- depth: float32 [1152, 18432], P('ny', 'nx'), may hold values from 0.5 to 2
- wet_mask: int32 [4, 1152, 18432], P(None, 'ny', 'nx'), may hold values 0 or 1
- shifts: int32 [4, 2], replicated, may hold values from 0 to 9, as said below
- parent_vals: float32 [4, 32768, 128], P(None, ('ny', 'nx')), may hold values from -3 to 3
- row_dest: int32 [4, 32768], P(None, ('ny', 'nx')), may hold values from 0 to 127, as said below
- row_coarse: int32 [4, 32768], P(None, ('ny', 'nx')), may hold values from 0 to 15
- edge_owner: int32 [4, 8], P(None, 'ny'), may hold values from 0 to 15
- edge_panels: float32 [4, 16, 1152], P(None, 'nx', 'ny'), may hold values from -8 to 8
Outputs:
- elevation_out: float32 [1152, 18432], P('ny', 'nx')
- flux_x_out: float32 [1152, 18432], P('ny', 'nx')
- flux_y_out: float32 [1152, 18432], P('ny', 'nx')
The draws below stay inside these ranges and needn't reach their ends.
Inputs may be any that keep to these rules, and one draw needn't show every extreme that they name: In every draw some step shifts the rows by 9 and some step shifts the columns by 9. `row_dest`: in each step, of the 256 rows of one device at most 8 name any one owner; in each step one owner is named by exactly 8 rows of every device.
All inputs are finite; a program needn't handle non-finite values. No bound on the sum of `wet_mask` on one device may be relied on, other than what follows from the above.
Results may differ from the reference program's by a relative error of at most 0.00014.
Values sent between devices are 32-bit elements; how exact they have to be, the bound alone decides.
No kernel may reach another device: no remote copies, remote signals or barrier semaphores. Data moves between devices by JAX's collectives and lax.ppermute only.
A program may use at most 128 MiB of HBM per device.

```python
import math
import jax
import jax.numpy as jnp
from jax import lax

RATIO = 9
CYC = 16
PW = 128
STEPS = 4
SH = 9
PR_DEV = 256
CAP = 8
CY = 144
CX = 1152
NYG = 1152
NXG = 18432
OWNERS = 128
PRT = 32768
N_NY = 8
N_NX = 16


def draw_shifts(key, part):
    first_key, row_key, col_key = jax.random.split(key, 3)
    base_shifts = jax.random.randint(first_key, (STEPS, 2), 0, SH + 1).astype(jnp.int32)
    row_step = jax.random.randint(row_key, (), 0, STEPS)
    col_step = jax.random.randint(col_key, (), 0, STEPS)
    base_shifts = base_shifts.at[row_step, 0].set(SH)
    return base_shifts.at[col_step, 1].set(SH).astype(jnp.int32)


def draw_row_dest(key, part):
    star_key, block_key = jax.random.split(key)
    stars = jax.random.randint(star_key, (STEPS,), 0, OWNERS).astype(jnp.int32)

    def one_block(block_seed, star_owner):
        pick_key, order_key = jax.random.split(block_seed)
        picked = jax.random.permutation(pick_key, (OWNERS - 1) * CAP)[:PR_DEV - CAP].astype(jnp.int32)
        other_owners = picked // CAP
        other_owners = other_owners + (other_owners >= star_owner).astype(jnp.int32)
        full_rows = jnp.zeros((CAP,), jnp.int32) + star_owner
        all_rows = jnp.concatenate([full_rows, other_owners.astype(jnp.int32)])
        return jax.random.permutation(order_key, all_rows)
    block_seeds = jax.random.split(block_key, STEPS * OWNERS)
    star_rows = jnp.repeat(stars, OWNERS)
    drawn = jax.vmap(one_block)(block_seeds, star_rows)
    return drawn.reshape(STEPS, OWNERS * PR_DEV).astype(jnp.int32)


def set_ends(values, own_key, low, high):
    place = [jax.random.randint(jax.random.fold_in(own_key, axis), (), 0, length) for axis, length in enumerate(values.shape)]
    longest = values.shape.index(max(values.shape))
    neighbour = place[:longest] + [(place[longest] + 1) % values.shape[longest]] + place[longest + 1:]
    return values.at[tuple(place)].set(low).at[tuple(neighbour)].set(high)


def block_levels(stream_key, dims, pieces, low, high):
    factor_of, own = 1.0, jax.random.fold_in(stream_key, 6)
    for axis_at, shards_of in pieces:
        draws = jnp.exp(jax.random.uniform(jax.random.fold_in(own, axis_at), (shards_of,), jnp.float32, low / len(pieces), high / len(pieces)))
        factor_of = factor_of * jnp.repeat(draws, dims[axis_at] // shards_of).reshape([-1 if axis == axis_at else 1 for axis in range(len(dims))])
    return factor_of


def centred(key, extent, scale, most, shards=(), kind=jnp.bfloat16):
    array = scale * jax.random.normal(key, extent, jnp.float32)
    if shards:
        array = array * block_levels(key, extent, shards, -0.22, 0.18)
    return jnp.clip(array, -most, most).astype(kind)


def setup_inputs(seed: int = 0) -> dict:
    arg_keys = jax.random.split(jax.random.key(seed), 12)
    elevation = centred(arg_keys[0], (NYG, NXG), 1.0, 6.0, ((0, 8), (1, 16)), jnp.float32)
    flux_x = centred(arg_keys[1], (NYG, NXG), 0.5, 3.0, ((0, 8), (1, 16)), jnp.float32)
    flux_y = centred(arg_keys[2], (NYG, NXG), 0.5, 3.0, ((0, 8), (1, 16)), jnp.float32)
    depth = jnp.clip(jnp.exp(math.log(2.0) - 1.3862944 * jax.random.uniform(arg_keys[3], (NYG, NXG), jnp.float32) ** block_levels(arg_keys[3], (NYG, NXG), ((0, 8), (1, 16)), -0.2, 0.2)), 0.5, 2.0)
    wet_mask = set_ends((jax.random.randint(arg_keys[4], (STEPS, NYG, NXG), 0, 5) < 4).astype(jnp.int32), jax.random.fold_in(arg_keys[4], 1), 0, 1)
    shifts = draw_shifts(jax.random.fold_in(arg_keys[11], 71), 0)
    parent_vals = centred(arg_keys[6], (STEPS, PRT, PW), 0.5, 3.0, ((1, 128),), jnp.float32)
    row_dest = draw_row_dest(jax.random.fold_in(arg_keys[11], 71), 0)
    row_coarse = set_ends(jax.random.randint(arg_keys[8], (STEPS, PRT), 0, CYC), jax.random.fold_in(arg_keys[8], 1), 0, CYC - 1).astype(jnp.int32)
    edge_owner = set_ends(jax.random.randint(arg_keys[9], (STEPS, N_NY), 0, N_NX), jax.random.fold_in(arg_keys[9], 1), 0, N_NX - 1).astype(jnp.int32)
    edge_panels = centred(arg_keys[10], (STEPS, N_NX, NYG), 2.0, 8.0, ((1, 16), (2, 8)), jnp.float32)
    return dict(elevation=elevation, flux_x=flux_x, flux_y=flux_y, depth=depth, wet_mask=wet_mask, shifts=shifts, parent_vals=parent_vals, row_dest=row_dest, row_coarse=row_coarse, edge_owner=edge_owner, edge_panels=edge_panels)


diffuse = 0.25
step_gain = 0.25


def interp_matrix(fine_count, coarse_count):
    fine_index = jnp.arange(fine_count, dtype=jnp.int32)
    numerator = 2 * fine_index + 1 - RATIO
    lower_index = jnp.clip(numerator // (2 * RATIO), 0, coarse_count - 2)
    weight = jnp.clip((numerator - lower_index * 2 * RATIO).astype(jnp.float32) / (2.0 * RATIO), 0.0, 1.0)
    coarse_index = jnp.arange(coarse_count, dtype=jnp.int32)
    at_lower = jnp.where(coarse_index[None, :] == lower_index[:, None], 1.0 - weight[:, None], 0.0)
    at_upper = jnp.where(coarse_index[None, :] == lower_index[:, None] + 1, weight[:, None], 0.0)
    return at_lower + at_upper


def west_of(grid_field):
    return grid_field[1:-1, :-1]


def east_of(grid_field):
    return grid_field[1:-1, 1:]


def south_of(grid_field):
    return grid_field[:-1, 1:-1]


def north_of(grid_field):
    return grid_field[1:, 1:-1]


def change(across, along):
    return across[:, 1:] - across[:, :-1] + along[1:, :] - along[:-1, :]


def advance(padded, depth_pad):
    surface, flow_x, flow_y, wetness = padded[0], padded[1], padded[2], padded[3]
    open_x = west_of(wetness) * east_of(wetness)
    mass_x = open_x * (0.5 * (west_of(flow_x) + east_of(flow_x)) - diffuse * (east_of(surface) - west_of(surface)))
    push_x = open_x * (0.25 * (west_of(depth_pad) + east_of(depth_pad)) * (west_of(surface) + east_of(surface)) - diffuse * (east_of(flow_x) - west_of(flow_x)))
    shear_x = open_x * (-diffuse * (east_of(flow_y) - west_of(flow_y)))
    open_y = south_of(wetness) * north_of(wetness)
    mass_y = open_y * (0.5 * (south_of(flow_y) + north_of(flow_y)) - diffuse * (north_of(surface) - south_of(surface)))
    push_y = open_y * (0.25 * (south_of(depth_pad) + north_of(depth_pad)) * (south_of(surface) + north_of(surface)) - diffuse * (north_of(flow_y) - south_of(flow_y)))
    shear_y = open_y * (-diffuse * (north_of(flow_x) - south_of(flow_x)))
    inner = wetness[1:-1, 1:-1]
    new_surface = surface[1:-1, 1:-1] - step_gain * change(mass_x, mass_y)
    new_flow_x = inner * (flow_x[1:-1, 1:-1] - step_gain * change(push_x, shear_y))
    new_flow_y = inner * (flow_y[1:-1, 1:-1] - step_gain * change(shear_x, push_y))
    return new_surface, new_flow_x, new_flow_y


def reference(elevation, flux_x, flux_y, depth, wet_mask, shifts, parent_vals, row_dest, row_coarse, edge_owner, edge_panels):
    rows_interp = interp_matrix(CY, CYC)
    cols_interp = interp_matrix(CX, PW)
    current = jnp.stack([elevation, flux_x, flux_y])
    depth_pad = jnp.pad(depth, 1)
    blocks = jnp.arange(N_NY, dtype=jnp.int32)
    for step_index in range(STEPS):
        widened = jnp.pad(current, ((0, 0), (0, SH), (0, SH)))
        shifted = lax.dynamic_slice(widened, (jnp.zeros((), jnp.int32), shifts[step_index, 0], shifts[step_index, 1]), (3, NYG, NXG))
        segment_ids = (row_dest[step_index] * CYC + row_coarse[step_index]).astype(jnp.int32)
        forcing_coarse = jax.ops.segment_sum(parent_vals[step_index], segment_ids, num_segments=OWNERS * CYC)
        forcing_coarse = forcing_coarse.reshape(N_NY, N_NX, CYC, PW)
        row_section = jnp.einsum("ic,abcp->aibp", rows_interp, forcing_coarse, precision=lax.Precision.HIGHEST)
        fine_forcing = jnp.einsum("aibp,jp->aibj", row_section, cols_interp, precision=lax.Precision.HIGHEST).reshape(NYG, NXG)
        raised = shifted[0] + fine_forcing
        edge_values = edge_panels[step_index].reshape(N_NX, N_NY, CY)[edge_owner[step_index], blocks].reshape(NYG)
        stacked = jnp.stack([raised, shifted[1], shifted[2], wet_mask[step_index].astype(jnp.float32)])
        padded = jnp.pad(stacked, ((0, 0), (1, 1), (1, 1)))
        padded = padded.at[0, 1:-1, 0].set(edge_values).at[3, 1:-1, 0].set(1.0)
        current = jnp.stack(advance(padded, depth_pad))
    return current[0], current[1], current[2]
```

```python
import functools

import jax
import jax.numpy as jnp
from jax import lax
from jax.experimental import pallas as pl
from jax.experimental.pallas import tpu as pltpu
from jax.sharding import PartitionSpec as P

RATIO = 9
STEPS = 4
CAP = 8
COARSE = 16
LANES = 128
ROWS, COLS = 144, 1152
FR, FC = 152, 1280
ROW0, COL0 = 4, 40
NHALO = 40
WIDTHS = (32, 24, 16, 8)
N_E, N_B, N_M = 0, 120, (152, 184, 208, 224)
N_ROWS, S_ROWS = 232, 64
CHUNK = 40
KTILE = COLS // LANES
E_PLACE = ((0, 0), (0, 40), (0, 80), (1, 0), (1, 64), (2, 0), (2, 32), (1, 32), (1, 88), (2, 16), (2, 40))
E_WIDTH = (40, 40, 40, 32, 24, 16, 8, 32, 24, 16, 8)

F32, BF16, I32 = jnp.float32, jnp.bfloat16, jnp.int32
VMEM = pl.BlockSpec(memory_space=pltpu.VMEM)
SMEM = pl.BlockSpec(memory_space=pltpu.SMEM)


def iota(shape, dim):
    return lax.broadcasted_iota(I32, shape, dim)


def left_over(shifts_ref, step, dim):
    total = jnp.int32(0)
    for later in range(STEPS):
        total += jnp.where(later > step, shifts_ref[later, dim], 0)
    return total


def halves(x):
    high = x.astype(BF16)
    return high, (x - high.astype(F32)).astype(BF16)


def dot(a, b, dims=((1,), (0,))):
    return lax.dot_general(a, b, (dims, ((), ())), preferred_element_type=F32)


def pack_kernel(dest_ref, dest_col_ref, coarse_col_ref, vals_ref, edge_ref, out_ref):
    owners = out_ref.shape[0]
    count = dest_ref.shape[1]
    before = iota((count, count), 0) < iota((count, count), 1)
    lane = iota((count, LANES), 1)
    place_row = iota((owners * CAP, count), 0)
    meta = jnp.zeros((owners * CAP, LANES), F32)
    for s in range(STEPS):
        dest = dest_ref[s : s + 1, :]
        same = (dest_col_ref[:, s : s + 1] == dest) & before
        slot = jnp.sum(jnp.where(same, 1.0, 0.0), axis=0, keepdims=True).astype(I32)
        hits = jnp.where(place_row == dest * CAP + slot, 1.0, 0.0).astype(BF16)
        high, low = halves(vals_ref[s])
        target = jnp.where(lane == s, coarse_col_ref[:, s : s + 1] + 1, 0).astype(F32).astype(BF16)
        out_ref[:, s * CAP : (s + 1) * CAP, :] = (dot(hits, high) + dot(hits, low)).reshape(
            owners, CAP, LANES
        )
        meta += dot(hits, target)
    out_ref[:, STEPS * CAP :, :] = meta.reshape(owners, CAP, LANES) + edge_ref[...][None]


def receive_kernel(got_ref, coarse_ref, edge_ref):
    sources = got_ref.shape[0]
    meta = got_ref[:, STEPS * CAP :, :].reshape(sources * CAP, LANES)
    lane = iota((sources * CAP, LANES), 1)
    for s in range(STEPS):
        target = meta[:, s : s + 1].astype(I32) - 1
        hits = jnp.where(lane == target, 1.0, 0.0).astype(BF16)
        high, low = halves(got_ref[:, s * CAP : (s + 1) * CAP, :].reshape(sources * CAP, LANES))
        both = ((0,), (0,))
        coarse_ref[s] = (dot(hits, high, both) + dot(hits, low, both))[:COARSE]
    row_block, col_groups = lax.axis_index("ny"), lax.axis_size("nx")
    for k in range(3):
        block = jnp.clip(row_block + k - 1, 0, lax.axis_size("ny") - 1)
        edge_ref[k] = jnp.sum(
            got_ref[pl.ds(block * col_groups, col_groups), STEPS * CAP :, :], axis=0
        )


def edge_flags():
    row_block, col_block = lax.axis_index("ny"), lax.axis_index("nx")
    south = jnp.where(row_block == 0, 0.0, 1.0).astype(F32)
    north = jnp.where(row_block == lax.axis_size("ny") - 1, 0.0, 1.0).astype(F32)
    west = jnp.where(col_block == 0, 0.0, 1.0).astype(F32)
    east = jnp.where(col_block == lax.axis_size("nx") - 1, 0.0, 1.0).astype(F32)
    return south, north, west, east


def fill_rows(tall_ref, own, south_ref, field, north_ref, north_at, width, flags):
    south, north = flags[0], flags[1]
    tall_ref[0:8, :] = south_ref[8 * field : 8 * field + 8, :] * south
    tall_ref[8 : 8 + ROWS, :] = own
    tall_ref[8 + ROWS : 8 + ROWS + width, :] = north_ref[north_at : north_at + width, :] * north


def window(tall_ref, row_shift, lanes):
    start = row_shift + ROW0
    base = pl.multiple_of((start >> 3) << 3, 8)
    tall = tall_ref[pl.ds(base, FR + 8), lanes]
    return pltpu.roll(tall, FR + 8 - (start & 7), 0)[:FR]


def pack_sides_kernel(
    shifts_ref, e_ref, u_ref, v_ref, b_ref, m_ref, north_ref, south_ref, out_ref, tall_ref
):
    side = pl.program_id(0)
    flags = edge_flags()
    lane = iota((FR, LANES), 1)
    tall_ref[...] = jnp.zeros_like(tall_ref)
    fields = []
    for f, ref in enumerate((e_ref, u_ref, v_ref)):
        fill_rows(tall_ref, ref[...], south_ref, f, north_ref, N_E + NHALO * f, NHALO, flags)
        fields.append(window(tall_ref, left_over(shifts_ref, -1, 0), slice(None)))
    fill_rows(tall_ref, b_ref[...], south_ref, 3, north_ref, N_B, WIDTHS[0], flags)
    for s in range(STEPS):
        fields.append(window(tall_ref, left_over(shifts_ref, s, 0), slice(None)))
    for s in range(STEPS):
        own = m_ref[s].astype(F32)
        fill_rows(tall_ref, own, south_ref, 4 + s, north_ref, N_M[s], WIDTHS[s], flags)
        fields.append(window(tall_ref, left_over(shifts_ref, s, 0), slice(None)))

    @pl.when(side == 0)
    def _():
        tiles = [jnp.zeros((FR, LANES), F32)] * 3
        for x, (tile, at), width in zip(fields, E_PLACE, E_WIDTH):
            moved = pltpu.roll(x, at, 1) if at else x
            tiles[tile] = jnp.where((lane >= at) & (lane < at + width), moved, tiles[tile])
        for k in range(3):
            out_ref[0, k] = tiles[k]

    @pl.when(side == 1)
    def _():
        tile = jnp.zeros((FR, LANES), F32)
        for f, x in enumerate(fields):
            moved = pltpu.roll(x, 8 * f + 8, 1)
            tile = jnp.where((lane >= 8 * f) & (lane < 8 * f + 8), moved, tile)
        out_ref[0, 0] = tile
        out_ref[0, 1] = tile
        out_ref[0, 2] = tile


def side_tiles(east_ref, west_ref, which, flags):
    tile, at = E_PLACE[which]
    right = east_ref[tile]
    if at:
        right = pltpu.roll(right, LANES - at, 1)
    left = pltpu.roll(west_ref[...], 120 - 8 * which, 1)
    return left * flags[2], right * flags[3]


def framed(tall_ref, row_shift, col_shift, left, right, write):
    lane = iota((FR, LANES), 1)
    turn = 128 - COL0 + col_shift
    amount = LANES - turn
    keep = lane < amount
    this = pltpu.roll(left, amount, 1)
    for k in range(FC // LANES):
        lanes = slice(k * LANES, (k + 1) * LANES)
        following = window(tall_ref, row_shift, lanes) if k < KTILE else right
        following = pltpu.roll(following, amount, 1)
        write(k, jnp.where(keep, this, following))
        this = following


def divide_18(n):
    return (n * 3641) >> 16


def prepare_kernel(
    shifts_ref, e_ref, u_ref, v_ref, b_ref, m_ref, north_ref, south_ref, east_ref, west_ref,
    state_ref, coef_ref, cols_ref, tall_ref, wet_ref, deep_ref, side_ref,
):
    s = pl.program_id(0)
    flags = edge_flags()
    is_west = lax.axis_index("nx") == 0

    @pl.when(s == 0)
    def _():
        tall_ref[...] = jnp.zeros_like(tall_ref)
        wet_ref[...] = jnp.zeros_like(wet_ref)
        deep_ref[...] = jnp.zeros_like(deep_ref)
        row_all, col_all = left_over(shifts_ref, -1, 0), left_over(shifts_ref, -1, 1)
        for f, ref in enumerate((e_ref, u_ref, v_ref)):
            fill_rows(tall_ref, ref[...], south_ref, f, north_ref, N_E + NHALO * f, NHALO, flags)

            def write(k, x, f=f):
                state_ref[f, :, k * LANES : (k + 1) * LANES] = x

            left, right = side_tiles(east_ref, west_ref, f, flags)
            framed(tall_ref, row_all, col_all, left, right, write)

    row_left, col_left = left_over(shifts_ref, s, 0), left_over(shifts_ref, s, 1)
    for step in range(STEPS):

        @pl.when(s == step)
        def _(step=step):
            side_ref[0], side_ref[1] = side_tiles(east_ref, west_ref, 3 + step, flags)
            side_ref[2], side_ref[3] = side_tiles(east_ref, west_ref, 7 + step, flags)

    fill_rows(tall_ref, b_ref[...], south_ref, 3, north_ref, N_B, WIDTHS[0], flags)

    def write_depth(k, x):
        deep_ref[0:FR, k * LANES : (k + 1) * LANES] = x

    framed(tall_ref, row_left, col_left, side_ref[0], side_ref[1], write_depth)

    for step in range(STEPS):

        @pl.when(s == step)
        def _(step=step):
            own = m_ref[0].astype(F32)
            fill_rows(
                tall_ref, own, south_ref, 4 + step, north_ref, N_M[step], WIDTHS[step], flags
            )

    row = iota((FR, LANES), 0)
    nest_row = lax.axis_index("ny") * ROWS + row + row_left - ROW0
    in_nest = (nest_row >= 0) & (nest_row < ROWS * lax.axis_size("ny"))
    lane = iota((FR, LANES), 1)
    ghost = in_nest & (lane == COL0 - 1 - col_left) & is_west

    def write_wet(k, x):
        coef_ref[0, 4, :, k * LANES : (k + 1) * LANES] = x
        wet_ref[0:FR, k * LANES : (k + 1) * LANES] = jnp.where(ghost, 1.0, x) if k == 0 else x

    framed(tall_ref, row_left, col_left, side_ref[2], side_ref[3], write_wet)

    for at in range(0, FR, 8):
        tile, above = slice(at, at + 8), slice(at + 1, at + 9)
        wet, deep = wet_ref[tile, :], deep_ref[tile, :]
        open_x = 0.0625 * wet * pltpu.roll(wet, FC - 1, 1)
        open_y = 0.0625 * wet * wet_ref[above, :]
        coef_ref[0, 0, tile, :] = open_x
        coef_ref[0, 1, tile, :] = open_x * (deep + pltpu.roll(deep, FC - 1, 1))
        coef_ref[0, 2, tile, :] = open_y
        coef_ref[0, 3, tile, :] = open_y * (deep + deep_ref[above, :])

    col = iota((1, FC), 1) + col_left - COL0
    inside = jnp.where(col < 0, col + COLS, jnp.where(col >= COLS, col - COLS, col))
    numerator = 2 * inside + 1 - RATIO
    lower = jnp.clip(divide_18(numerator + 18) - 1, 0, LANES - 2)
    weight = jnp.clip(numerator - 18 * lower, 0, 18)
    first = lower + jnp.where((col < 0) | (col >= COLS), LANES, 0)
    for part in range(2):
        place = iota((LANES, FC), 0) + part * LANES
        cols_ref[0, part * LANES : (part + 1) * LANES, :] = jnp.where(
            place == first, 18 - weight, jnp.where(place == first + 1, weight, 0)
        ).astype(F32).astype(BF16)


def steps_kernel(
    shifts_ref, state_ref, coef_ref, cols_ref, own_ref, east_ref, west_ref, edge_ref,
    e_out, u_out, v_out, cur, rise, flow,
):
    s = pl.program_id(0)
    row_left, col_left = left_over(shifts_ref, s, 0), left_over(shifts_ref, s, 1)
    is_west = lax.axis_index("nx") == 0
    east = jnp.where(lax.axis_index("nx") == lax.axis_size("nx") - 1, 0.0, 1.0).astype(F32)

    @pl.when(s == 0)
    def _():
        for f in range(3):
            cur[f, 0:8, :] = jnp.zeros((8, FC), F32)
            cur[f, 8 : 8 + FR, :] = state_ref[f]
            cur[f, 8 + FR :, :] = jnp.zeros((8, FC), F32)
            flow[f] = jnp.zeros((16, FC), F32)

    i = iota((FR, 1), 0) + row_left - ROW0
    block = jnp.where(i < 0, 0, jnp.where(i >= ROWS, 2, 1))
    inside = i - (block - 1) * ROWS
    numerator = 2 * inside + 1 - RATIO
    lower = jnp.clip(divide_18(numerator + 18) - 1, 0, COARSE - 2)
    weight = jnp.clip(numerator - 18 * lower, 0, 18)
    first = lower + 16 * block - 8
    place = iota((FR, 32), 1)
    rows = jnp.where(place == first, 18 - weight, jnp.where(place == first + 1, weight, 0))
    rows = rows.astype(F32).astype(BF16)
    side = jnp.where(iota((32, LANES), 1) < 64, east_ref[0] * east, west_ref[0])
    total = 0.0
    parts = []
    for x in (own_ref[0], side):
        high, low = halves(x)
        parts.append(dot(rows, high) + dot(rows, low))
    section = jnp.concatenate(parts, axis=1) * (1.0 / 324.0)
    high, low = halves(section)
    rise[...] = dot(high, cols_ref[0]) + dot(low, cols_ref[0])

    half = jnp.where(inside >= 72, 1, 0)
    pick = jnp.where(iota((FR, 24), 1) == 8 * block + 2 * s + half, 1.0, 0.0).astype(BF16)
    high, low = halves(edge_ref[...].reshape(24, LANES))
    line = dot(pick, high) + dot(pick, low)
    lane = iota((FR, LANES), 1)
    edge = jnp.sum(jnp.where(lane == 8 + inside - 72 * half, line, 0.0), axis=1, keepdims=True)
    ghost = (lane == COL0 - 1 - col_left) & is_west

    cur[0, 8 : 8 + FR, :] += rise[...]
    cur[0, 8 : 8 + FR, 0:LANES] = jnp.where(ghost, edge, cur[0, 8 : 8 + FR, 0:LANES])
    cur[1, 8 : 8 + FR, 0:LANES] = jnp.where(ghost, 0.0, cur[1, 8 : 8 + FR, 0:LANES])
    cur[2, 8 : 8 + FR, 0:LANES] = jnp.where(ghost, 0.0, cur[2, 8 : 8 + FR, 0:LANES])

    def eastern(x):
        return pltpu.roll(x, FC - 1, 1)

    def net_x(x):
        return x - pltpu.roll(x, 1, 1)

    for at in range(0, FR, 8):
        own, above, tile = slice(at + 8, at + 16), slice(at + 9, at + 17), slice(at, at + 8)
        E, U, V = cur[0, own, :], cur[1, own, :], cur[2, own, :]
        bx, cx, by, cy = (coef_ref[0, k, tile, :] for k in range(4))
        inner = coef_ref[0, 4, tile, :]
        Ee, Ue, Ve = eastern(E), eastern(U), eastern(V)
        new_e = E - net_x(bx * (2.0 * (U + Ue) - (Ee - E)))
        new_u = U - net_x(cx * (E + Ee) - bx * (Ue - U))
        new_v = V + net_x(bx * (Ve - V))
        En, Un, Vn = cur[0, above, :], cur[1, above, :], cur[2, above, :]
        north = (
            by * (2.0 * (V + Vn) - (En - E)),
            by * (Un - U),
            cy * (E + En) - by * (Vn - V),
        )
        net = []
        for f in range(3):
            flow[f, 7:8, :] = flow[f, 15:16, :]
            flow[f, 8:16, :] = north[f]
            net.append(north[f] - flow[f, 7:15, :])
        cur[0, own, :] = new_e - net[0]
        cur[1, own, :] = inner * (new_u + net[1])
        cur[2, own, :] = inner * (new_v - net[2])

    @pl.when(s == STEPS - 1)
    def _():
        lane8 = iota((ROWS, LANES), 1)
        for f, ref in enumerate((e_out, u_out, v_out)):
            this = pltpu.roll(cur[f, 8 + ROW0 : 8 + ROW0 + ROWS, 0:LANES], LANES - COL0, 1)
            for k in range(KTILE):
                following = cur[f, 8 + ROW0 : 8 + ROW0 + ROWS, (k + 1) * LANES : (k + 2) * LANES]
                following = pltpu.roll(following, LANES - COL0, 1)
                ref[:, k * LANES : (k + 1) * LANES] = jnp.where(
                    lane8 < LANES - COL0, this, following
                )
                this = following


def ring(value, axis, by):
    count = lax.axis_size(axis)
    return lax.ppermute(value, axis, [(i, (i + by) % count) for i in range(count)])


def limits(mib, **more):
    return pltpu.CompilerParams(vmem_limit_bytes=mib * 1024 * 1024, **more)


def local(
    elevation, flux_x, flux_y, depth, wet_mask, shifts, parent_vals, row_dest, row_coarse,
    edge_owner, edge_panels,
):
    owners = lax.axis_size("ny") * lax.axis_size("nx")
    sds = jax.ShapeDtypeStruct
    wet = [wet_mask[s] for s in range(STEPS)]

    north_message = jnp.concatenate(
        [x[:NHALO] for x in (elevation, flux_x, flux_y)]
        + [depth[: WIDTHS[0]]]
        + [x[:w].astype(F32) for x, w in zip(wet, WIDTHS)]
    )
    south_message = jnp.concatenate(
        [x[-8:] for x in (elevation, flux_x, flux_y, depth)] + [x[-8:].astype(F32) for x in wet]
    )
    from_north = ring(north_message, "ny", -1)
    from_south = ring(south_message, "ny", 1)

    panel = jnp.where(edge_owner == lax.axis_index("nx"), edge_panels[:, 0, :], 0.0)
    panel = jnp.pad(panel.reshape(2 * STEPS, 72), ((0, 0), (8, 48)))
    send = pl.pallas_call(
        pack_kernel,
        out_shape=sds((owners, CHUNK, LANES), F32),
        in_specs=[VMEM] * 5,
        out_specs=VMEM,
        compiler_params=limits(40),
        cost_estimate=pl.CostEstimate(flops=800_000_000, bytes_accessed=3_200_000, transcendentals=0),
        name="pack_rows",
    )(row_dest, row_dest.T, row_coarse.T, parent_vals, panel)
    got = lax.all_to_all(send, ("ny", "nx"), split_axis=0, concat_axis=0, tiled=True)

    last = KTILE - 1
    pick = lambda g: (0, g * last)
    sides = pl.pallas_call(
        pack_sides_kernel,
        out_shape=sds((2, 3, FR, LANES), F32),
        grid=(2,),
        in_specs=[SMEM]
        + [pl.BlockSpec((ROWS, LANES), pick)] * 4
        + [pl.BlockSpec((STEPS, ROWS, LANES), lambda g: (0, 0, g * last))]
        + [pl.BlockSpec((N_ROWS, LANES), pick), pl.BlockSpec((S_ROWS, LANES), pick)],
        out_specs=pl.BlockSpec((1, 3, FR, LANES), lambda g: (g, 0, 0, 0)),
        scratch_shapes=[pltpu.VMEM((16 + ROWS + NHALO, LANES), F32)],
        compiler_params=limits(32),
        cost_estimate=pl.CostEstimate(flops=8_000_000, bytes_accessed=2_500_000, transcendentals=0),
        name="pack_sides",
    )(shifts, elevation, flux_x, flux_y, depth, wet_mask, from_north, from_south)
    from_east = ring(sides[0], "nx", -1)
    from_west = ring(sides[1, 0], "nx", 1)

    whole = lambda *shape: pl.BlockSpec(shape, lambda g: (0,) * len(shape))
    state, coef, cols = pl.pallas_call(
        prepare_kernel,
        out_shape=(
            sds((3, FR, FC), F32),
            sds((STEPS, 5, FR, FC), F32),
            sds((STEPS, 2 * LANES, FC), BF16),
        ),
        grid=(STEPS,),
        in_specs=[SMEM]
        + [whole(ROWS, COLS)] * 4
        + [pl.BlockSpec((1, ROWS, COLS), lambda g: (g, 0, 0))]
        + [whole(N_ROWS, COLS), whole(S_ROWS, COLS), whole(3, FR, LANES), whole(FR, LANES)],
        out_specs=(
            whole(3, FR, FC),
            pl.BlockSpec((1, 5, FR, FC), lambda g: (g, 0, 0, 0)),
            pl.BlockSpec((1, 2 * LANES, FC), lambda g: (g, 0, 0)),
        ),
        scratch_shapes=[
            pltpu.VMEM((16 + ROWS + NHALO, COLS), F32),
            pltpu.VMEM((FR + 8, FC), F32),
            pltpu.VMEM((FR + 8, FC), F32),
            pltpu.VMEM((4, FR, LANES), F32),
        ],
        compiler_params=limits(48),
        cost_estimate=pl.CostEstimate(
            flops=60_000_000, bytes_accessed=27_000_000, transcendentals=0
        ),
        name="prepare",
    )(
        shifts, elevation, flux_x, flux_y, depth, wet_mask, from_north, from_south,
        from_east, from_west,
    )

    coarse, edge = pl.pallas_call(
        receive_kernel,
        out_shape=(sds((STEPS, COARSE, LANES), F32), sds((3, CAP, LANES), F32)),
        in_specs=[VMEM],
        out_specs=(VMEM, VMEM),
        compiler_params=limits(40),
        cost_estimate=pl.CostEstimate(flops=300_000_000, bytes_accessed=2_700_000, transcendentals=0),
        name="receive_rows",
    )(got)
    coarse_north = ring(coarse, "ny", -1)
    coarse_south = ring(coarse, "ny", 1)
    north_flag = lax.axis_index("ny") < lax.axis_size("ny") - 1
    tall = jnp.concatenate(
        [coarse_south[:, 8:], coarse, jnp.where(north_flag, coarse_north[:, :8], 0.0)], axis=1
    )
    tall_east = ring(tall, "nx", -1)
    tall_west = ring(tall, "nx", 1)

    step_tall = pl.BlockSpec((1, 32, LANES), lambda g: (g, 0, 0))
    return pl.pallas_call(
        steps_kernel,
        out_shape=(sds((ROWS, COLS), F32),) * 3,
        grid=(STEPS,),
        in_specs=[
            SMEM,
            whole(3, FR, FC),
            pl.BlockSpec((1, 5, FR, FC), lambda g: (g, 0, 0, 0)),
            pl.BlockSpec((1, 2 * LANES, FC), lambda g: (g, 0, 0)),
            step_tall,
            step_tall,
            step_tall,
            whole(3, CAP, LANES),
        ],
        out_specs=(whole(ROWS, COLS),) * 3,
        scratch_shapes=[
            pltpu.VMEM((3, FR + 16, FC), F32),
            pltpu.VMEM((FR, FC), F32),
            pltpu.VMEM((3, 16, FC), F32),
        ],
        compiler_params=limits(48),
        cost_estimate=pl.CostEstimate(
            flops=400_000_000, bytes_accessed=23_000_000, transcendentals=0
        ),
        name="steps",
    )(shifts, state, coef, cols, tall, tall_east, tall_west, edge)


def solution(mesh):
    in_specs = (
        P("ny", "nx"),
        P("ny", "nx"),
        P("ny", "nx"),
        P("ny", "nx"),
        P(None, "ny", "nx"),
        P(),
        P(None, ("ny", "nx"), None),
        P(None, ("ny", "nx")),
        P(None, ("ny", "nx")),
        P(None, "ny"),
        P(None, "nx", "ny"),
    )
    out_specs = (P("ny", "nx"), P("ny", "nx"), P("ny", "nx"))
    return jax.shard_map(local, mesh=mesh, in_specs=in_specs, out_specs=out_specs, check_vma=False)
```

```python
import functools

import jax
import jax.numpy as jnp
from jax import lax
from jax.experimental import pallas as pl
from jax.experimental.pallas import tpu as pltpu
from jax.sharding import PartitionSpec as P

RATIO = 9
STEPS = 4
CAP = 8
COARSE = 16
LANES = 128
ROWS, COLS = 144, 1152
FR, FC = 152, 1280
ROW0, COL0 = 4, 40
NHALO = 40
WIDTHS = (32, 24, 16, 8)
N_E, N_B, N_M = 0, 120, (152, 184, 208, 224)
N_ROWS, S_ROWS = 232, 64
CHUNK = 40
PREPARE_MIB, STEPS_MIB = 63, 63
META = 124
KTILE, FTILE = COLS // LANES, FC // LANES
E_PLACE = ((0, 0), (0, 40), (0, 80), (1, 0), (1, 64), (2, 0), (2, 32), (1, 32), (1, 88), (2, 16), (2, 40))
E_WIDTH = (40, 40, 40, 32, 24, 16, 8, 32, 24, 16, 8)

F32, BF16, I32 = jnp.float32, jnp.bfloat16, jnp.int32
VMEM = pl.BlockSpec(memory_space=pltpu.VMEM)
SMEM = pl.BlockSpec(memory_space=pltpu.SMEM)


def iota(shape, dim):
    return lax.broadcasted_iota(I32, shape, dim)


def left_over(shifts_ref, step, dim):
    total = jnp.int32(0)
    for later in range(STEPS):
        total += jnp.where(later > step, shifts_ref[dim, later], 0)
    return total


def halves(x):
    high = x.astype(BF16)
    return high, (x - high.astype(F32)).astype(BF16)


def dot(a, b, dims=((1,), (0,))):
    return lax.dot_general(a, b, (dims, ((), ())), preferred_element_type=F32)


def message_kernel(
    e_top, u_top, v_top, b_top, m_top, e_low, u_low, v_low, b_low, m_low, north_ref, south_ref
):
    for f, ref in enumerate((e_top, u_top, v_top)):
        north_ref[N_E + NHALO * f : N_E + NHALO * (f + 1), :] = ref[...]
    north_ref[N_B : N_B + WIDTHS[0], :] = b_top[...]
    for f, ref in enumerate((e_low, u_low, v_low, b_low)):
        south_ref[8 * f : 8 * f + 8, :] = ref[...]
    for s in range(STEPS):
        north_ref[N_M[s] : N_M[s] + WIDTHS[s], :] = m_top[s, : WIDTHS[s], :].astype(F32)
        south_ref[32 + 8 * s : 40 + 8 * s, :] = m_low[s].astype(F32)


def pack_kernel(owner_ref, dest_ref, coarse_ref, vals_ref, panel_ref, after_ref, out_ref):
    del after_ref
    owners = out_ref.shape[0]
    count = dest_ref.shape[1]
    before = iota((count, count), 0) < iota((count, count), 1)
    unit = jnp.where(iota((count, count), 0) == iota((count, count), 1), 1.0, 0.0).astype(BF16)
    numbers = jnp.concatenate([dest_ref[...], coarse_ref[...] + 1], axis=0).astype(F32)
    upright = dot(unit, numbers.astype(BF16), ((1,), (1,)))
    lane = iota((count, LANES), 1)
    place_row = iota((owners * CAP, count), 0)
    meta = jnp.zeros((owners * CAP, LANES), F32)
    for s in range(STEPS):
        dest = dest_ref[s : s + 1, :]
        same = (upright[:, s : s + 1] == dest.astype(F32)) & before
        slot = jnp.sum(jnp.where(same, 1.0, 0.0), axis=0, keepdims=True).astype(I32)
        hits = jnp.where(place_row == dest * CAP + slot, 1.0, 0.0).astype(BF16)
        high, low = halves(vals_ref[s])
        target = jnp.where(lane == META + s, upright[:, STEPS + s : STEPS + s + 1], 0.0)
        out_ref[:, s * CAP : (s + 1) * CAP, :] = (dot(hits, high) + dot(hits, low)).reshape(
            owners, CAP, LANES
        )
        meta += dot(hits, target.astype(BF16))
    lane1 = iota((1, LANES), 1)
    first, second = [], []
    for s in range(STEPS):
        mine = owner_ref[0:1, s : s + 1] == lax.axis_index("nx")
        head = panel_ref[s, :, 0:LANES]
        tail = jnp.concatenate(
            [panel_ref[s, :, LANES:ROWS], jnp.zeros((1, 2 * LANES - ROWS), F32)], axis=1
        )
        first.append(jnp.where((lane1 < 120) & mine, head, 0.0))
        both = jnp.where(lane1 < 8, pltpu.roll(head, 8, 1), pltpu.roll(tail, 8, 1))
        second.append(jnp.where((lane1 < 24) & mine, both, 0.0))
    edges = jnp.concatenate(first + second, axis=0)
    out_ref[:, STEPS * CAP :, :] = meta.reshape(owners, CAP, LANES) + edges[None]


def receive_kernel(got_ref, after_ref, coarse_ref, edge_ref):
    del after_ref
    sources = got_ref.shape[0]
    meta = got_ref[:, STEPS * CAP :, :].reshape(sources * CAP, LANES)
    choose = jnp.where(iota((8, LANES), 1) == META + iota((8, LANES), 0), 1.0, 0.0)
    targets = dot(choose.astype(BF16), meta.astype(BF16), ((1,), (1,)))
    index = iota((COARSE, sources * CAP), 0)
    for s in range(STEPS):
        hits = jnp.where(index == targets[s : s + 1, :].astype(I32) - 1, 1.0, 0.0).astype(BF16)
        high, low = halves(got_ref[:, s * CAP : (s + 1) * CAP, :].reshape(sources * CAP, LANES))
        coarse_ref[s] = dot(hits, high) + dot(hits, low)
    row_block, col_groups = lax.axis_index("ny"), lax.axis_size("nx")
    for k in range(3):
        block = jnp.clip(row_block + k - 1, 0, lax.axis_size("ny") - 1)
        edge_ref[k] = jnp.sum(
            got_ref[pl.ds(block * col_groups, col_groups), STEPS * CAP :, :], axis=0
        )


def edge_flags():
    row_block, col_block = lax.axis_index("ny"), lax.axis_index("nx")
    south = jnp.where(row_block == 0, 0.0, 1.0).astype(F32)
    north = jnp.where(row_block == lax.axis_size("ny") - 1, 0.0, 1.0).astype(F32)
    west = jnp.where(col_block == 0, 0.0, 1.0).astype(F32)
    east = jnp.where(col_block == lax.axis_size("nx") - 1, 0.0, 1.0).astype(F32)
    return south, north, west, east


def fill_rows(tall_ref, own, south_ref, field, north_ref, north_at, width, flags):
    south, north = flags[0], flags[1]
    for k in range(tall_ref.shape[0]):
        lanes = slice(k * LANES, (k + 1) * LANES)
        tall_ref[k, 0:8, :] = south_ref[8 * field : 8 * field + 8, lanes] * south
        tall_ref[k, 8 : 8 + ROWS, :] = own(lanes)
        tall_ref[k, 8 + ROWS : 8 + ROWS + width, :] = (
            north_ref[north_at : north_at + width, lanes] * north
        )


def side_tiles(east_ref, west_ref, which, flags):
    tile, at = E_PLACE[which]
    right = east_ref[tile]
    if at:
        right = pltpu.roll(right, LANES - at, 1)
    left = pltpu.roll(west_ref[...], 120 - 8 * which, 1)
    return left * flags[2], right * flags[3]


def framed(ext, row_shift, col_shift, strips, write):
    lane = iota((FR, LANES), 1)
    turn = 128 - COL0 + col_shift
    amount = LANES - turn
    keep = lane < amount
    done, this = None, None
    for k in strips:
        if done != k:
            this = pltpu.roll(ext(k), amount, 1)
        following = pltpu.roll(ext(k + 1), amount, 1)
        write(k, jnp.where(keep, this, following))
        done, this = k + 1, following


def to_east(x, following, last_lane):
    return jnp.where(
        last_lane, pltpu.roll(following, LANES - 1, 1), pltpu.roll(x, LANES - 1, 1)
    )


def divide_18(n):
    return (n * 3641) >> 16


def frame_fields(
    shifts_ref, load, left_of, right_of, wet_ref, deep_ref,
    strips, state_to, coef_to, coef_strips, aside,
):
    def ext(which, tile_rows, row_shift):
        rows = pl.ds(row_shift + ROW0, FR)

        def tile(k):
            if k == 0:
                return left_of(which)
            if k == KTILE + 1:
                return right_of(which)
            return tile_rows(k - 1, rows)

        return tile

    row_all, col_all = left_over(shifts_ref, -1, 0), left_over(shifts_ref, -1, 1)
    for f in range(3):
        tiles = ext(f, load(f), row_all)
        aside(f, tiles)
        framed(tiles, row_all, col_all, coef_strips, functools.partial(state_to, f))
    wet_ref[:, FR:, :] = jnp.zeros_like(wet_ref[:, FR:, :])
    deep_ref[:, FR:, :] = jnp.zeros_like(deep_ref[:, FR:, :])
    last_lane = iota((8, LANES), 1) == LANES - 1
    row, lane = iota((FR, LANES), 0), iota((FR, LANES), 1)
    is_west = lax.axis_index("nx") == 0
    tile_rows = load(3)
    for s in range(STEPS):
        row_left, col_left = left_over(shifts_ref, s, 0), left_over(shifts_ref, s, 1)

        def write_depth(k, x, s=s):
            deep_ref[s * FTILE + k, 0:FR, :] = x

        tiles = ext(3 + s, tile_rows, row_left)
        aside(3 + s, tiles)
        framed(tiles, row_left, col_left, strips, write_depth)
    for s in range(STEPS):
        row_left, col_left = left_over(shifts_ref, s, 0), left_over(shifts_ref, s, 1)
        tiles = ext(7 + s, load(4 + s), row_left)
        aside(7 + s, tiles)
        nest_row = lax.axis_index("ny") * ROWS + row + row_left - ROW0
        in_nest = (nest_row >= 0) & (nest_row < ROWS * lax.axis_size("ny"))
        ghost = in_nest & (lane == COL0 - 1 - col_left) & is_west

        def write_wet(k, x, s=s, ghost=ghost):
            if k in coef_strips:
                coef_to(s, 4, k, slice(0, FR), x)
            wet_ref[k, 0:FR, :] = jnp.where(ghost, 1.0, x) if k == 0 else x

        framed(tiles, row_left, col_left, strips, write_wet)
        for k in coef_strips:
            east = min(k + 1, FTILE - 1)
            for at in range(0, FR, 8):
                tile, above = slice(at, at + 8), slice(at + 1, at + 9)
                wet, deep = wet_ref[k, tile, :], deep_ref[s * FTILE + k, tile, :]
                wet_e = to_east(wet, wet_ref[east, tile, :], last_lane)
                deep_e = to_east(deep, deep_ref[s * FTILE + east, tile, :], last_lane)
                wet = 0.0625 * wet
                open_x = wet * wet_e
                open_y = wet * wet_ref[k, above, :]
                coef_to(s, 0, k, tile, open_x)
                coef_to(s, 1, k, tile, open_x * (deep + deep_e))
                coef_to(s, 2, k, tile, open_y)
                coef_to(s, 3, k, tile, open_y * (deep + deep_ref[s * FTILE + k, above, :]))


def prepare_kernel(
    shifts_ref, e_ref, u_ref, v_ref, b_ref, m_ref, north_ref, south_ref,
    state_ref, coef_ref, cols_ref, ends_ref, east_ref, west_ref, tall_ref, wet_ref, deep_ref,
):
    flags = edge_flags()
    own_of = [lambda lanes, ref=ref: ref[:, lanes] for ref in (e_ref, u_ref, v_ref, b_ref)]
    own_of += [lambda lanes, s=s: m_ref[s, :, lanes].astype(F32) for s in range(STEPS)]
    starts = (N_E, N_E + NHALO, N_E + 2 * NHALO, N_B, *N_M)
    widths = (NHALO,) * 3 + (WIDTHS[0],) + WIDTHS
    lane = iota((FR, LANES), 1)
    tall_ref[...] = jnp.zeros_like(tall_ref)
    east_ref[...] = jnp.zeros_like(east_ref)
    west_ref[...] = jnp.zeros_like(west_ref)

    def load(field):
        fill_rows(
            tall_ref, own_of[field], south_ref, field, north_ref, starts[field], widths[field], flags
        )
        for place, k in enumerate((0, 1, KTILE - 1)):
            ends_ref[field, place] = tall_ref[k]
        return lambda k, rows: tall_ref[k, rows, :]

    def aside(which, tiles):
        (tile, at), width = E_PLACE[which], E_WIDTH[which]
        moved = pltpu.roll(tiles(1), at, 1) if at else tiles(1)
        east_ref[tile] = jnp.where((lane >= at) & (lane < at + width), moved, east_ref[tile])
        at = 8 * which
        moved = pltpu.roll(tiles(KTILE), at + 8, 1)
        west_ref[...] = jnp.where((lane >= at) & (lane < at + 8), moved, west_ref[...])

    def none(which):
        return jnp.zeros((FR, LANES), F32)

    def state_to(f, k, x):
        state_ref[f, k - 1] = x

    def coef_to(s, c, k, rows, x):
        coef_ref[s, c, k - 1, rows, :] = x

    frame_fields(
        shifts_ref, load, none, none, wet_ref, deep_ref,
        range(1, FTILE), state_to, coef_to, range(1, FTILE - 1), aside,
    )
    for s in range(STEPS):
        col = iota((1, FC), 1) + left_over(shifts_ref, s, 1) - COL0
        inside = jnp.where(col < 0, col + COLS, jnp.where(col >= COLS, col - COLS, col))
        numerator = 2 * inside + 1 - RATIO
        lower = jnp.clip(divide_18(numerator + 18) - 1, 0, LANES - 2)
        weight = jnp.clip(numerator - 18 * lower, 0, 18)
        first = lower + jnp.where((col < 0) | (col >= COLS), LANES, 0)
        for part in range(2):
            place = iota((LANES, FC), 0) + part * LANES
            cols_ref[s, part * LANES : (part + 1) * LANES, :] = jnp.where(
                place == first, 18 - weight, jnp.where(place == first + 1, weight, 0)
            ).astype(F32).astype(BF16)


def side_strips_kernel(
    shifts_ref, ends_ref, east_ref, west_ref, after_ref, state_ref, coef_ref, wet_ref, deep_ref
):
    del after_ref
    flags = edge_flags()

    def load(field):
        return lambda k, rows: ends_ref[field, min(k, 2), rows, :]

    def state_to(f, k, x):
        state_ref[f, 1 if k else 0] = x

    def coef_to(s, c, k, rows, x):
        coef_ref[s, c, 1 if k else 0, rows, :] = x

    frame_fields(
        shifts_ref,
        load,
        lambda which: side_tiles(east_ref, west_ref, which, flags)[0],
        lambda which: side_tiles(east_ref, west_ref, which, flags)[1],
        wet_ref,
        deep_ref,
        (0, 1, FTILE - 1),
        state_to,
        coef_to,
        (0, FTILE - 1),
        lambda which, tiles: None,
    )


def one_step(
    s, shifts_ref, mid_ref, side_ref, cols_ref, own_ref, east_ref, west_ref, edge_ref, cur, new
):
    row_left, col_left = left_over(shifts_ref, s, 0), left_over(shifts_ref, s, 1)
    is_west = lax.axis_index("nx") == 0
    east = jnp.where(lax.axis_index("nx") == lax.axis_size("nx") - 1, 0.0, 1.0).astype(F32)

    i = iota((FR, 1), 0) + row_left - ROW0
    block = jnp.where(i < 0, 0, jnp.where(i >= ROWS, 2, 1))
    inside = i - (block - 1) * ROWS
    numerator = 2 * inside + 1 - RATIO
    lower = jnp.clip(divide_18(numerator + 18) - 1, 0, COARSE - 2)
    weight = jnp.clip(numerator - 18 * lower, 0, 18)
    first = lower + 16 * block - 8
    place = iota((FR, 32), 1)
    rows = jnp.where(place == first, 18 - weight, jnp.where(place == first + 1, weight, 0))
    rows = rows.astype(F32).astype(BF16)
    side = jnp.where(iota((32, LANES), 1) < 64, east_ref[s] * east, west_ref[s])
    parts = []
    for x in (own_ref[s], side):
        high, low = halves(x)
        parts.append(dot(rows, high) + dot(rows, low))
    section = jnp.concatenate(parts, axis=1) * (1.0 / 324.0)
    high, low = halves(section)
    for k in range(0, FTILE, 2):
        lanes = slice(k * LANES, (k + 2) * LANES)
        rise = dot(high, cols_ref[s, :, lanes]) + dot(low, cols_ref[s, :, lanes])
        cur[0, k, 0:FR, :] += rise[:, :LANES]
        cur[0, k + 1, 0:FR, :] += rise[:, LANES:]

    half = jnp.where(inside >= 120, 1, 0)
    pick = jnp.where(iota((FR, 24), 1) == 8 * block + 4 * half + s, 1.0, 0.0).astype(BF16)
    high, low = halves(edge_ref[...].reshape(24, LANES))
    line = dot(pick, high) + dot(pick, low)
    lane = iota((FR, LANES), 1)
    edge = jnp.sum(jnp.where(lane == inside - 120 * half, line, 0.0), axis=1, keepdims=True)
    ghost = (lane == COL0 - 1 - col_left) & is_west

    cur[0, 0, 0:FR, :] = jnp.where(ghost, edge, cur[0, 0, 0:FR, :])
    cur[1, 0, 0:FR, :] = jnp.where(ghost, 0.0, cur[1, 0, 0:FR, :])
    cur[2, 0, 0:FR, :] = jnp.where(ghost, 0.0, cur[2, 0, 0:FR, :])
    def cat(f, rows):
        return jnp.concatenate([cur[f, k, rows, :] for k in range(FTILE)], axis=1)

    def coefficient(c, rows):
        tiles = [mid_ref[s, c, k, rows, :] for k in range(FTILE - 2)]
        ends = [side_ref[s, c, k, rows, :] for k in range(2)]
        return jnp.concatenate([ends[0], *tiles, ends[1]], axis=1)

    first_row = iota((8, FC), 0) == 0
    south = [jnp.zeros((8, FC), F32)] * 3
    for at in range(0, FR, 8):
        tile, above = slice(at, at + 8), slice(at + 1, at + 9)
        E, U, V = (cat(f, tile) for f in range(3))
        Ee, Ue, Ve = (pltpu.roll(x, FC - 1, 1) for x in (E, U, V))
        bx, cx, by, cy, inner = (coefficient(c, tile) for c in range(5))
        across = (
            bx * (2.0 * (U + Ue) - (Ee - E)),
            cx * (E + Ee) - bx * (Ue - U),
            bx * (V - Ve),
        )
        out = [x - (a - pltpu.roll(a, 1, 1)) for x, a in zip((E, U, V), across)]
        En, Un, Vn = (cat(f, above) for f in range(3))
        along = (
            by * (2.0 * (V + Vn) - (En - E)),
            by * (U - Un),
            cy * (E + En) - by * (Vn - V),
        )
        for f in range(3):
            lifted = pltpu.roll(along[f], 1, 0)
            out[f] = out[f] - (along[f] - jnp.where(first_row, south[f], lifted))
            south[f] = lifted
        out = (out[0], inner * out[1], inner * out[2])
        for f in range(3):
            for k in range(FTILE):
                new[f, k, tile, :] = out[f][:, k * LANES : (k + 1) * LANES]


def steps_kernel(
    shifts_ref, mid_state, side_state, mid_hbm, side_hbm, cols_hbm, own_ref, east_ref, west_ref,
    edge_ref, e_out, u_out, v_out, even, odd, mid_ref, side_ref, cols_ref, sems,
):
    copies = []
    for f in range(3):
        copies.append(
            pltpu.make_async_copy(
                mid_state.at[f], even.at[f, 1 : FTILE - 1, 0:FR, :], sems.at[f]
            )
        )
        for end, k in enumerate((0, FTILE - 1)):
            copies.append(
                pltpu.make_async_copy(
                    side_state.at[f, end], even.at[f, k, 0:FR, :], sems.at[3 + 2 * f + end]
                )
            )
    per_step = []
    for s in range(STEPS):
        pairs = ((cols_hbm, cols_ref), (mid_hbm, mid_ref), (side_hbm, side_ref))
        per_step.append(
            [
                pltpu.make_async_copy(a.at[s], b.at[s], sems.at[9 + 3 * s + i])
                for i, (a, b) in enumerate(pairs)
            ]
        )
    for copy in copies:
        copy.start()
    for each in per_step:
        for copy in each:
            copy.start()
    for f in range(3):
        for k in range(FTILE):
            even[f, k, FR:, :] = jnp.zeros((8, LANES), F32)
            odd[f, k, FR:, :] = jnp.zeros((8, LANES), F32)
    for copy in copies:
        copy.wait()
    cur, new = even, odd
    for s in range(STEPS):
        for copy in per_step[s]:
            copy.wait()
        one_step(
            s, shifts_ref, mid_ref, side_ref, cols_ref, own_ref, east_ref, west_ref, edge_ref,
            cur, new,
        )
        cur, new = new, cur
    keep = iota((ROWS, LANES), 1) < LANES - COL0
    rows = slice(ROW0, ROW0 + ROWS)
    for f, ref in enumerate((e_out, u_out, v_out)):
        this = pltpu.roll(cur[f, 0, rows, :], LANES - COL0, 1)
        for k in range(KTILE):
            following = pltpu.roll(cur[f, k + 1, rows, :], LANES - COL0, 1)
            ref[:, k * LANES : (k + 1) * LANES] = jnp.where(keep, this, following)
            this = following


def ring(value, axis, by):
    count = lax.axis_size(axis)
    return lax.ppermute(value, axis, [(i, (i + by) % count) for i in range(count)])


def limits(mib, **more):
    return pltpu.CompilerParams(vmem_limit_bytes=mib * 1024 * 1024, **more)


def local(
    elevation, flux_x, flux_y, depth, wet_mask, shifts, parent_vals, row_dest, row_coarse,
    edge_owner, edge_panels,
):
    shifts = shifts.T
    owners = lax.axis_size("ny") * lax.axis_size("nx")
    sds = jax.ShapeDtypeStruct
    top = lambda rows: pl.BlockSpec((rows, COLS), lambda g: (0, 0))
    low = pl.BlockSpec((8, COLS), lambda g: (ROWS // 8 - 1, 0))
    fields = (elevation, flux_x, flux_y, depth, wet_mask)
    north_message, south_message = pl.pallas_call(
        message_kernel,
        out_shape=(sds((N_ROWS, COLS), F32), sds((S_ROWS, COLS), F32)),
        grid=(1,),
        in_specs=[top(NHALO)] * 3
        + [top(WIDTHS[0]), pl.BlockSpec((STEPS, WIDTHS[0], COLS), lambda g: (0, 0, 0))]
        + [low] * 4
        + [pl.BlockSpec((STEPS, 8, COLS), lambda g: (0, ROWS // 8 - 1, 0))],
        out_specs=(top(N_ROWS), top(S_ROWS)),
        compiler_params=limits(63),
        cost_estimate=pl.CostEstimate(flops=300_000, bytes_accessed=2_700_000, transcendentals=0),
        name="messages",
    )(*fields, *fields)
    from_north = ring(north_message, "ny", -1)
    from_south = ring(south_message, "ny", 1)

    send = pl.pallas_call(
        pack_kernel,
        out_shape=sds((owners, CHUNK, LANES), F32),
        in_specs=[VMEM] * 5 + [pl.BlockSpec(memory_space=pl.ANY)],
        out_specs=VMEM,
        compiler_params=limits(63),
        cost_estimate=pl.CostEstimate(flops=800_000_000, bytes_accessed=3_200_000, transcendentals=0),
        name="pack_rows",
    )(edge_owner.reshape(1, STEPS), row_dest, row_coarse, parent_vals, edge_panels, south_message)
    send, from_south, from_north = lax.optimization_barrier((send, from_south, from_north))
    got = lax.all_to_all(send, ("ny", "nx"), split_axis=0, concat_axis=0, tiled=True)

    frame = lambda *lead: sds((*lead, FR, LANES), F32)
    tall_rows = 16 + ROWS + NHALO
    mid_state, mid_coef, cols, ends, east_side, west_side = pl.pallas_call(
        prepare_kernel,
        out_shape=(
            frame(3, FTILE - 2),
            frame(STEPS, 5, FTILE - 2),
            sds((STEPS, 2 * LANES, FC), BF16),
            sds((4 + STEPS, 3, tall_rows, LANES), F32),
            frame(3),
            frame(),
        ),
        in_specs=[SMEM] + [VMEM] * 7,
        out_specs=(VMEM,) * 6,
        scratch_shapes=[
            pltpu.VMEM((KTILE, tall_rows, LANES), F32),
            pltpu.VMEM((FTILE, FR + 8, LANES), F32),
            pltpu.VMEM((STEPS * FTILE, FR + 8, LANES), F32),
        ],
        compiler_params=limits(PREPARE_MIB),
        cost_estimate=pl.CostEstimate(
            flops=60_000_000, bytes_accessed=27_000_000, transcendentals=0
        ),
        name="prepare",
    )(shifts, *fields, from_north, from_south)
    from_east = ring(east_side, "nx", -1)
    from_west = ring(west_side, "nx", 1)

    coarse, edge = pl.pallas_call(
        receive_kernel,
        out_shape=(sds((STEPS, COARSE, LANES), F32), sds((3, CAP, LANES), F32)),
        in_specs=[VMEM, pl.BlockSpec(memory_space=pl.ANY)],
        out_specs=(VMEM, VMEM),
        compiler_params=limits(63),
        cost_estimate=pl.CostEstimate(flops=300_000_000, bytes_accessed=2_700_000, transcendentals=0),
        name="receive_rows",
    )(got, ends)
    coarse_north = ring(coarse, "ny", -1)
    coarse_south = ring(coarse, "ny", 1)
    north_flag = lax.axis_index("ny") < lax.axis_size("ny") - 1
    tall = jnp.concatenate(
        [coarse_south[:, 8:], coarse, jnp.where(north_flag, coarse_north[:, :8], 0.0)], axis=1
    )

    side_state, side_coef = pl.pallas_call(
        side_strips_kernel,
        out_shape=(frame(3, 2), frame(STEPS, 5, 2)),
        in_specs=[SMEM] + [VMEM] * 3 + [pl.BlockSpec(memory_space=pl.ANY)],
        out_specs=(VMEM, VMEM),
        scratch_shapes=[
            pltpu.VMEM((FTILE, FR + 8, LANES), F32),
            pltpu.VMEM((STEPS * FTILE, FR + 8, LANES), F32),
        ],
        compiler_params=limits(PREPARE_MIB),
        cost_estimate=pl.CostEstimate(flops=12_000_000, bytes_accessed=6_000_000, transcendentals=0),
        name="side_strips",
    )(shifts, ends, from_east, from_west, coarse)
    tall_east = ring(tall, "nx", -1)
    tall_west = ring(tall, "nx", 1)

    return pl.pallas_call(
        steps_kernel,
        out_shape=(sds((ROWS, COLS), F32),) * 3,
        in_specs=[SMEM] + [pl.BlockSpec(memory_space=pl.ANY)] * 5 + [VMEM] * 4,
        out_specs=(VMEM,) * 3,
        scratch_shapes=[
            pltpu.VMEM((3, FTILE, FR + 8, LANES), F32),
            pltpu.VMEM((3, FTILE, FR + 8, LANES), F32),
            pltpu.VMEM((STEPS, 5, FTILE - 2, FR, LANES), F32),
            pltpu.VMEM((STEPS, 5, 2, FR, LANES), F32),
            pltpu.VMEM((STEPS, 2 * LANES, FC), BF16),
            pltpu.SemaphoreType.DMA((9 + 3 * STEPS,)),
        ],
        compiler_params=limits(STEPS_MIB),
        cost_estimate=pl.CostEstimate(
            flops=400_000_000, bytes_accessed=23_000_000, transcendentals=0
        ),
        name="steps",
    )(shifts, mid_state, side_state, mid_coef, side_coef, cols, tall, tall_east, tall_west, edge)


def solution(mesh):
    in_specs = (
        P("ny", "nx"),
        P("ny", "nx"),
        P("ny", "nx"),
        P("ny", "nx"),
        P(None, "ny", "nx"),
        P(),
        P(None, ("ny", "nx"), None),
        P(None, ("ny", "nx")),
        P(None, ("ny", "nx")),
        P(None, "ny"),
        P(None, "nx", "ny"),
    )
    out_specs = (P("ny", "nx"), P("ny", "nx"), P("ny", "nx"))
    return jax.shard_map(local, mesh=mesh, in_specs=in_specs, out_specs=out_specs, check_vma=False)
```

```python
import functools

import jax
import jax.numpy as jnp
from jax import lax
from jax.experimental import pallas as pl
from jax.experimental.pallas import tpu as pltpu
from jax.sharding import PartitionSpec as P

RATIO = 9
STEPS = 4
CAP = 8
COARSE = 16
LANES = 128
ROWS, COLS = 144, 1152
FR, FC = 152, 1280
ROW0, COL0 = 4, 40
NHALO = 40
WIDTHS = (32, 24, 16, 8)
N_E, N_B, N_M = 0, 120, (152, 184, 208, 224)
N_ROWS, S_ROWS = 232, 64
CHUNK = 40
PREPARE_MIB, STEPS_MIB = 63, 63
META = 124
KTILE, FTILE = COLS // LANES, FC // LANES
E_PLACE = ((0, 0), (0, 40), (0, 80), (1, 0), (1, 64), (2, 0), (2, 32), (1, 32), (1, 88), (2, 16), (2, 40))
E_WIDTH = (40, 40, 40, 32, 24, 16, 8, 32, 24, 16, 8)

F32, BF16, I32 = jnp.float32, jnp.bfloat16, jnp.int32
VMEM = pl.BlockSpec(memory_space=pltpu.VMEM)
SMEM = pl.BlockSpec(memory_space=pltpu.SMEM)


def iota(shape, dim):
    return lax.broadcasted_iota(I32, shape, dim)


def left_over(shifts_ref, step, dim):
    total = jnp.int32(0)
    for later in range(STEPS):
        total += jnp.where(later > step, shifts_ref[dim, later], 0)
    return total


def halves(x):
    high = x.astype(BF16)
    return high, (x - high.astype(F32)).astype(BF16)


def dot(a, b, dims=((1,), (0,))):
    return lax.dot_general(a, b, (dims, ((), ())), preferred_element_type=F32)


def message_kernel(
    e_top, u_top, v_top, b_top, m_top, e_low, u_low, v_low, b_low, m_low, north_ref, south_ref
):
    for f, ref in enumerate((e_top, u_top, v_top)):
        north_ref[N_E + NHALO * f : N_E + NHALO * (f + 1), :] = ref[...]
    north_ref[N_B : N_B + WIDTHS[0], :] = b_top[...]
    for f, ref in enumerate((e_low, u_low, v_low, b_low)):
        south_ref[8 * f : 8 * f + 8, :] = ref[...]
    for s in range(STEPS):
        north_ref[N_M[s] : N_M[s] + WIDTHS[s], :] = m_top[s, : WIDTHS[s], :].astype(F32)
        south_ref[32 + 8 * s : 40 + 8 * s, :] = m_low[s].astype(F32)


def pack_kernel(owner_ref, dest_ref, coarse_ref, vals_ref, panel_ref, after_ref, out_ref):
    del after_ref
    owners = out_ref.shape[0]
    count = dest_ref.shape[1]
    before = iota((count, count), 0) < iota((count, count), 1)
    unit = jnp.where(iota((count, count), 0) == iota((count, count), 1), 1.0, 0.0).astype(BF16)
    numbers = jnp.concatenate([dest_ref[...], coarse_ref[...] + 1], axis=0).astype(F32)
    upright = dot(unit, numbers.astype(BF16), ((1,), (1,)))
    lane = iota((count, LANES), 1)
    place_row = iota((owners * CAP, count), 0)
    meta = jnp.zeros((owners * CAP, LANES), F32)
    for s in range(STEPS):
        dest = dest_ref[s : s + 1, :]
        same = (upright[:, s : s + 1] == dest.astype(F32)) & before
        slot = jnp.sum(jnp.where(same, 1.0, 0.0), axis=0, keepdims=True).astype(I32)
        hits = jnp.where(place_row == dest * CAP + slot, 1.0, 0.0).astype(BF16)
        high, low = halves(vals_ref[s])
        target = jnp.where(lane == META + s, upright[:, STEPS + s : STEPS + s + 1], 0.0)
        out_ref[:, s * CAP : (s + 1) * CAP, :] = (dot(hits, high) + dot(hits, low)).reshape(
            owners, CAP, LANES
        )
        meta += dot(hits, target.astype(BF16))
    lane1 = iota((1, LANES), 1)
    first, second = [], []
    for s in range(STEPS):
        mine = owner_ref[0:1, s : s + 1] == lax.axis_index("nx")
        head = panel_ref[s, :, 0:LANES]
        tail = jnp.concatenate(
            [panel_ref[s, :, LANES:ROWS], jnp.zeros((1, 2 * LANES - ROWS), F32)], axis=1
        )
        first.append(jnp.where((lane1 < 120) & mine, head, 0.0))
        both = jnp.where(lane1 < 8, pltpu.roll(head, 8, 1), pltpu.roll(tail, 8, 1))
        second.append(jnp.where((lane1 < 24) & mine, both, 0.0))
    edges = jnp.concatenate(first + second, axis=0)
    out_ref[:, STEPS * CAP :, :] = meta.reshape(owners, CAP, LANES) + edges[None]


def receive_kernel(got_ref, after_ref, coarse_ref, edge_ref):
    del after_ref
    sources = got_ref.shape[0]
    meta = got_ref[:, STEPS * CAP :, :].reshape(sources * CAP, LANES)
    choose = jnp.where(iota((8, LANES), 1) == META + iota((8, LANES), 0), 1.0, 0.0)
    targets = dot(choose.astype(BF16), meta.astype(BF16), ((1,), (1,)))
    index = iota((COARSE, sources * CAP), 0)
    for s in range(STEPS):
        hits = jnp.where(index == targets[s : s + 1, :].astype(I32) - 1, 1.0, 0.0).astype(BF16)
        high, low = halves(got_ref[:, s * CAP : (s + 1) * CAP, :].reshape(sources * CAP, LANES))
        coarse_ref[s] = dot(hits, high) + dot(hits, low)
    row_block, col_groups = lax.axis_index("ny"), lax.axis_size("nx")
    for k in range(3):
        block = jnp.clip(row_block + k - 1, 0, lax.axis_size("ny") - 1)
        edge_ref[k] = jnp.sum(
            got_ref[pl.ds(block * col_groups, col_groups), STEPS * CAP :, :], axis=0
        )


def edge_flags():
    row_block, col_block = lax.axis_index("ny"), lax.axis_index("nx")
    south = jnp.where(row_block == 0, 0.0, 1.0).astype(F32)
    north = jnp.where(row_block == lax.axis_size("ny") - 1, 0.0, 1.0).astype(F32)
    west = jnp.where(col_block == 0, 0.0, 1.0).astype(F32)
    east = jnp.where(col_block == lax.axis_size("nx") - 1, 0.0, 1.0).astype(F32)
    return south, north, west, east


def fill_rows(tall_ref, own, south_ref, field, north_ref, north_at, width, flags):
    south, north = flags[0], flags[1]
    for k in range(tall_ref.shape[0]):
        lanes = slice(k * LANES, (k + 1) * LANES)
        tall_ref[k, 0:8, :] = south_ref[8 * field : 8 * field + 8, lanes] * south
        tall_ref[k, 8 : 8 + ROWS, :] = own(lanes)
        tall_ref[k, 8 + ROWS : 8 + ROWS + width, :] = (
            north_ref[north_at : north_at + width, lanes] * north
        )


def side_tiles(east_ref, west_ref, which, flags):
    tile, at = E_PLACE[which]
    right = east_ref[tile]
    if at:
        right = pltpu.roll(right, LANES - at, 1)
    left = pltpu.roll(west_ref[...], 120 - 8 * which, 1)
    return left * flags[2], right * flags[3]


def framed(ext, row_shift, col_shift, strips, write):
    lane = iota((FR, LANES), 1)
    turn = 128 - COL0 + col_shift
    amount = LANES - turn
    keep = lane < amount
    done, this = None, None
    for k in strips:
        if done != k:
            this = pltpu.roll(ext(k), amount, 1)
        following = pltpu.roll(ext(k + 1), amount, 1)
        write(k, jnp.where(keep, this, following))
        done, this = k + 1, following


def to_east(x, following, last_lane):
    return jnp.where(
        last_lane, pltpu.roll(following, LANES - 1, 1), pltpu.roll(x, LANES - 1, 1)
    )


def divide_18(n):
    return (n * 3641) >> 16


def frame_fields(
    shifts_ref, load, left_of, right_of, wet_ref, deep_ref,
    strips, state_to, coef_to, coef_strips, aside,
):
    def ext(which, tile_rows, row_shift):
        rows = pl.ds(row_shift + ROW0, FR)

        def tile(k):
            if k == 0:
                return left_of(which)
            if k == KTILE + 1:
                return right_of(which)
            return tile_rows(k - 1, rows)

        return tile

    row_all, col_all = left_over(shifts_ref, -1, 0), left_over(shifts_ref, -1, 1)
    for f in range(3):
        tiles = ext(f, load(f), row_all)
        aside(f, tiles)
        framed(tiles, row_all, col_all, coef_strips, functools.partial(state_to, f))
    wet_ref[:, FR:, :] = jnp.zeros_like(wet_ref[:, FR:, :])
    deep_ref[:, FR:, :] = jnp.zeros_like(deep_ref[:, FR:, :])
    last_lane = iota((8, LANES), 1) == LANES - 1
    row, lane = iota((FR, LANES), 0), iota((FR, LANES), 1)
    is_west = lax.axis_index("nx") == 0
    tile_rows = load(3)
    for s in range(STEPS):
        row_left, col_left = left_over(shifts_ref, s, 0), left_over(shifts_ref, s, 1)

        def write_depth(k, x, s=s):
            deep_ref[s * FTILE + k, 0:FR, :] = x

        tiles = ext(3 + s, tile_rows, row_left)
        aside(3 + s, tiles)
        framed(tiles, row_left, col_left, strips, write_depth)
    for s in range(STEPS):
        row_left, col_left = left_over(shifts_ref, s, 0), left_over(shifts_ref, s, 1)
        tiles = ext(7 + s, load(4 + s), row_left)
        aside(7 + s, tiles)
        nest_row = lax.axis_index("ny") * ROWS + row + row_left - ROW0
        in_nest = (nest_row >= 0) & (nest_row < ROWS * lax.axis_size("ny"))
        ghost = in_nest & (lane == COL0 - 1 - col_left) & is_west

        def write_wet(k, x, s=s, ghost=ghost):
            if k in coef_strips:
                coef_to(s, 4, k, slice(0, FR), x)
            wet_ref[k, 0:FR, :] = jnp.where(ghost, 1.0, x) if k == 0 else x

        framed(tiles, row_left, col_left, strips, write_wet)
        for k in coef_strips:
            east = min(k + 1, FTILE - 1)
            for at in range(0, FR, 8):
                tile, above = slice(at, at + 8), slice(at + 1, at + 9)
                wet, deep = wet_ref[k, tile, :], deep_ref[s * FTILE + k, tile, :]
                wet_e = to_east(wet, wet_ref[east, tile, :], last_lane)
                deep_e = to_east(deep, deep_ref[s * FTILE + east, tile, :], last_lane)
                wet = 0.0625 * wet
                open_x = wet * wet_e
                open_y = wet * wet_ref[k, above, :]
                coef_to(s, 0, k, tile, open_x)
                coef_to(s, 1, k, tile, open_x * (deep + deep_e))
                coef_to(s, 2, k, tile, open_y)
                coef_to(s, 3, k, tile, open_y * (deep + deep_ref[s * FTILE + k, above, :]))


def prepare_kernel(
    shifts_ref, e_ref, u_ref, v_ref, b_ref, m_ref, north_ref, south_ref,
    state_ref, coef_ref, cols_ref, ends_ref, east_ref, west_ref, tall_ref, wet_ref, deep_ref,
):
    flags = edge_flags()
    own_of = [lambda lanes, ref=ref: ref[:, lanes] for ref in (e_ref, u_ref, v_ref, b_ref)]
    own_of += [lambda lanes, s=s: m_ref[s, :, lanes].astype(F32) for s in range(STEPS)]
    starts = (N_E, N_E + NHALO, N_E + 2 * NHALO, N_B, *N_M)
    widths = (NHALO,) * 3 + (WIDTHS[0],) + WIDTHS
    lane = iota((FR, LANES), 1)
    tall_ref[...] = jnp.zeros_like(tall_ref)
    east_ref[...] = jnp.zeros_like(east_ref)
    west_ref[...] = jnp.zeros_like(west_ref)

    def load(field):
        fill_rows(
            tall_ref, own_of[field], south_ref, field, north_ref, starts[field], widths[field], flags
        )
        for place, k in enumerate((0, 1, KTILE - 1)):
            ends_ref[field, place] = tall_ref[k]
        return lambda k, rows: tall_ref[k, rows, :]

    def aside(which, tiles):
        (tile, at), width = E_PLACE[which], E_WIDTH[which]
        moved = pltpu.roll(tiles(1), at, 1) if at else tiles(1)
        east_ref[tile] = jnp.where((lane >= at) & (lane < at + width), moved, east_ref[tile])
        at = 8 * which
        moved = pltpu.roll(tiles(KTILE), at + 8, 1)
        west_ref[...] = jnp.where((lane >= at) & (lane < at + 8), moved, west_ref[...])

    def none(which):
        return jnp.zeros((FR, LANES), F32)

    def state_to(f, k, x):
        state_ref[f, k - 1] = x

    def coef_to(s, c, k, rows, x):
        coef_ref[s, c, k - 1, rows, :] = x

    frame_fields(
        shifts_ref, load, none, none, wet_ref, deep_ref,
        range(1, FTILE), state_to, coef_to, range(1, FTILE - 1), aside,
    )
    for s in range(STEPS):
        col = iota((1, FC), 1) + left_over(shifts_ref, s, 1) - COL0
        inside = jnp.where(col < 0, col + COLS, jnp.where(col >= COLS, col - COLS, col))
        numerator = 2 * inside + 1 - RATIO
        lower = jnp.clip(divide_18(numerator + 18) - 1, 0, LANES - 2)
        weight = jnp.clip(numerator - 18 * lower, 0, 18)
        first = lower + jnp.where((col < 0) | (col >= COLS), LANES, 0)
        for part in range(2):
            place = iota((LANES, FC), 0) + part * LANES
            cols_ref[s, part * LANES : (part + 1) * LANES, :] = jnp.where(
                place == first, 18 - weight, jnp.where(place == first + 1, weight, 0)
            ).astype(F32).astype(BF16)


def side_strips_kernel(
    shifts_ref, ends_ref, east_ref, west_ref, after_ref, state_ref, coef_ref, wet_ref, deep_ref
):
    del after_ref
    flags = edge_flags()

    def load(field):
        return lambda k, rows: ends_ref[field, min(k, 2), rows, :]

    def state_to(f, k, x):
        state_ref[f, 1 if k else 0] = x

    def coef_to(s, c, k, rows, x):
        coef_ref[s, c, 1 if k else 0, rows, :] = x

    frame_fields(
        shifts_ref,
        load,
        lambda which: side_tiles(east_ref, west_ref, which, flags)[0],
        lambda which: side_tiles(east_ref, west_ref, which, flags)[1],
        wet_ref,
        deep_ref,
        (0, 1, FTILE - 1),
        state_to,
        coef_to,
        (0, FTILE - 1),
        lambda which, tiles: None,
    )


def one_step(
    s, shifts_ref, mid_ref, side_ref, cols_ref, own_ref, east_ref, west_ref, edge_ref, cur, new
):
    row_left, col_left = left_over(shifts_ref, s, 0), left_over(shifts_ref, s, 1)
    is_west = lax.axis_index("nx") == 0
    east = jnp.where(lax.axis_index("nx") == lax.axis_size("nx") - 1, 0.0, 1.0).astype(F32)

    i = iota((FR, 1), 0) + row_left - ROW0
    block = jnp.where(i < 0, 0, jnp.where(i >= ROWS, 2, 1))
    inside = i - (block - 1) * ROWS
    numerator = 2 * inside + 1 - RATIO
    lower = jnp.clip(divide_18(numerator + 18) - 1, 0, COARSE - 2)
    weight = jnp.clip(numerator - 18 * lower, 0, 18)
    first = lower + 16 * block - 8
    place = iota((FR, 32), 1)
    rows = jnp.where(place == first, 18 - weight, jnp.where(place == first + 1, weight, 0))
    rows = rows.astype(F32).astype(BF16)
    side = jnp.where(iota((32, LANES), 1) < 64, east_ref[s] * east, west_ref[s])
    parts = []
    for x in (own_ref[s], side):
        high, low = halves(x)
        parts.append(dot(rows, high) + dot(rows, low))
    section = jnp.concatenate(parts, axis=1) * (1.0 / 324.0)
    high, low = halves(section)
    for k in range(0, FTILE, 2):
        lanes = slice(k * LANES, (k + 2) * LANES)
        rise = dot(high, cols_ref[s, :, lanes]) + dot(low, cols_ref[s, :, lanes])
        cur[0, k, 0:FR, :] += rise[:, :LANES]
        cur[0, k + 1, 0:FR, :] += rise[:, LANES:]

    half = jnp.where(inside >= 120, 1, 0)
    pick = jnp.where(iota((FR, 24), 1) == 8 * block + 4 * half + s, 1.0, 0.0).astype(BF16)
    high, low = halves(edge_ref[...].reshape(24, LANES))
    line = dot(pick, high) + dot(pick, low)
    lane = iota((FR, LANES), 1)
    edge = jnp.sum(jnp.where(lane == inside - 120 * half, line, 0.0), axis=1, keepdims=True)
    ghost = (lane == COL0 - 1 - col_left) & is_west

    cur[0, 0, 0:FR, :] = jnp.where(ghost, edge, cur[0, 0, 0:FR, :])
    cur[1, 0, 0:FR, :] = jnp.where(ghost, 0.0, cur[1, 0, 0:FR, :])
    cur[2, 0, 0:FR, :] = jnp.where(ghost, 0.0, cur[2, 0, 0:FR, :])
    def cat(f, rows):
        return jnp.concatenate([cur[f, k, rows, :] for k in range(FTILE)], axis=1)

    def coefficient(c, rows):
        tiles = [mid_ref[s, c, k, rows, :] for k in range(FTILE - 2)]
        ends = [side_ref[s, c, k, rows, :] for k in range(2)]
        return jnp.concatenate([ends[0], *tiles, ends[1]], axis=1)

    first_row = iota((8, FC), 0) == 0
    south = [jnp.zeros((8, FC), F32)] * 3
    for at in range(0, FR, 8):
        tile, above = slice(at, at + 8), slice(at + 1, at + 9)
        E, U, V = (cat(f, tile) for f in range(3))
        Ee, Ue, Ve = (pltpu.roll(x, FC - 1, 1) for x in (E, U, V))
        bx, cx, by, cy, inner = (coefficient(c, tile) for c in range(5))
        across = (
            bx * (2.0 * (U + Ue) - (Ee - E)),
            cx * (E + Ee) - bx * (Ue - U),
            bx * (V - Ve),
        )
        out = [x - (a - pltpu.roll(a, 1, 1)) for x, a in zip((E, U, V), across)]
        En, Un, Vn = (cat(f, above) for f in range(3))
        along = (
            by * (2.0 * (V + Vn) - (En - E)),
            by * (U - Un),
            cy * (E + En) - by * (Vn - V),
        )
        for f in range(3):
            lifted = pltpu.roll(along[f], 1, 0)
            out[f] = out[f] - (along[f] - jnp.where(first_row, south[f], lifted))
            south[f] = lifted
        out = (out[0], inner * out[1], inner * out[2])
        for f in range(3):
            for k in range(FTILE):
                new[f, k, tile, :] = out[f][:, k * LANES : (k + 1) * LANES]


def steps_kernel(
    shifts_ref, mid_state, side_state, mid_hbm, side_hbm, cols_hbm, own_ref, east_ref, west_ref,
    edge_ref, e_out, u_out, v_out, even, odd, mid_ref, side_ref, cols_ref, sems,
):
    copies = []
    for f in range(3):
        copies.append(
            pltpu.make_async_copy(
                mid_state.at[f], even.at[f, 1 : FTILE - 1, 0:FR, :], sems.at[f]
            )
        )
        for end, k in enumerate((0, FTILE - 1)):
            copies.append(
                pltpu.make_async_copy(
                    side_state.at[f, end], even.at[f, k, 0:FR, :], sems.at[3 + 2 * f + end]
                )
            )
    per_step = []
    for s in range(STEPS):
        pairs = ((cols_hbm, cols_ref), (mid_hbm, mid_ref), (side_hbm, side_ref))
        per_step.append(
            [
                pltpu.make_async_copy(a.at[s], b.at[s], sems.at[9 + 3 * s + i])
                for i, (a, b) in enumerate(pairs)
            ]
        )
    for copy in copies:
        copy.start()
    for copy in per_step[0]:
        copy.start()
    for f in range(3):
        for k in range(FTILE):
            even[f, k, FR:, :] = jnp.zeros((8, LANES), F32)
            odd[f, k, FR:, :] = jnp.zeros((8, LANES), F32)
    for copy in copies:
        copy.wait()
    cur, new = even, odd
    for s in range(STEPS):
        for copy in per_step[s]:
            copy.wait()
        if s + 1 < STEPS:
            for copy in per_step[s + 1]:
                copy.start()
        one_step(
            s, shifts_ref, mid_ref, side_ref, cols_ref, own_ref, east_ref, west_ref, edge_ref,
            cur, new,
        )
        cur, new = new, cur
    keep = iota((ROWS, LANES), 1) < LANES - COL0
    rows = slice(ROW0, ROW0 + ROWS)
    for f, ref in enumerate((e_out, u_out, v_out)):
        this = pltpu.roll(cur[f, 0, rows, :], LANES - COL0, 1)
        for k in range(KTILE):
            following = pltpu.roll(cur[f, k + 1, rows, :], LANES - COL0, 1)
            ref[:, k * LANES : (k + 1) * LANES] = jnp.where(keep, this, following)
            this = following


def ring(value, axis, by):
    count = lax.axis_size(axis)
    return lax.ppermute(value, axis, [(i, (i + by) % count) for i in range(count)])


def limits(mib, **more):
    return pltpu.CompilerParams(vmem_limit_bytes=mib * 1024 * 1024, **more)


def local(
    elevation, flux_x, flux_y, depth, wet_mask, shifts, parent_vals, row_dest, row_coarse,
    edge_owner, edge_panels,
):
    shifts = shifts.T
    owners = lax.axis_size("ny") * lax.axis_size("nx")
    sds = jax.ShapeDtypeStruct
    top = lambda rows: pl.BlockSpec((rows, COLS), lambda g: (0, 0))
    low = pl.BlockSpec((8, COLS), lambda g: (ROWS // 8 - 1, 0))
    fields = (elevation, flux_x, flux_y, depth, wet_mask)
    north_message, south_message = pl.pallas_call(
        message_kernel,
        out_shape=(sds((N_ROWS, COLS), F32), sds((S_ROWS, COLS), F32)),
        grid=(1,),
        in_specs=[top(NHALO)] * 3
        + [top(WIDTHS[0]), pl.BlockSpec((STEPS, WIDTHS[0], COLS), lambda g: (0, 0, 0))]
        + [low] * 4
        + [pl.BlockSpec((STEPS, 8, COLS), lambda g: (0, ROWS // 8 - 1, 0))],
        out_specs=(top(N_ROWS), top(S_ROWS)),
        compiler_params=limits(63),
        cost_estimate=pl.CostEstimate(flops=300_000, bytes_accessed=2_700_000, transcendentals=0),
        name="messages",
    )(*fields, *fields)
    from_north = ring(north_message, "ny", -1)
    from_south = ring(south_message, "ny", 1)

    send = pl.pallas_call(
        pack_kernel,
        out_shape=sds((owners, CHUNK, LANES), F32),
        in_specs=[VMEM] * 5 + [pl.BlockSpec(memory_space=pl.ANY)],
        out_specs=VMEM,
        compiler_params=limits(63),
        cost_estimate=pl.CostEstimate(flops=800_000_000, bytes_accessed=3_200_000, transcendentals=0),
        name="pack_rows",
    )(edge_owner.reshape(1, STEPS), row_dest, row_coarse, parent_vals, edge_panels, south_message)
    send, from_south, from_north = lax.optimization_barrier((send, from_south, from_north))
    got = lax.all_to_all(send, ("ny", "nx"), split_axis=0, concat_axis=0, tiled=True)

    frame = lambda *lead: sds((*lead, FR, LANES), F32)
    tall_rows = 16 + ROWS + NHALO
    mid_state, mid_coef, cols, ends, east_side, west_side = pl.pallas_call(
        prepare_kernel,
        out_shape=(
            frame(3, FTILE - 2),
            frame(STEPS, 5, FTILE - 2),
            sds((STEPS, 2 * LANES, FC), BF16),
            sds((4 + STEPS, 3, tall_rows, LANES), F32),
            frame(3),
            frame(),
        ),
        in_specs=[SMEM] + [VMEM] * 7,
        out_specs=(VMEM,) * 6,
        scratch_shapes=[
            pltpu.VMEM((KTILE, tall_rows, LANES), F32),
            pltpu.VMEM((FTILE, FR + 8, LANES), F32),
            pltpu.VMEM((STEPS * FTILE, FR + 8, LANES), F32),
        ],
        compiler_params=limits(PREPARE_MIB),
        cost_estimate=pl.CostEstimate(
            flops=60_000_000, bytes_accessed=27_000_000, transcendentals=0
        ),
        name="prepare",
    )(shifts, *fields, from_north, from_south)
    from_east = ring(east_side, "nx", -1)
    from_west = ring(west_side, "nx", 1)

    coarse, edge = pl.pallas_call(
        receive_kernel,
        out_shape=(sds((STEPS, COARSE, LANES), F32), sds((3, CAP, LANES), F32)),
        in_specs=[VMEM, pl.BlockSpec(memory_space=pl.ANY)],
        out_specs=(VMEM, VMEM),
        compiler_params=limits(63),
        cost_estimate=pl.CostEstimate(flops=300_000_000, bytes_accessed=2_700_000, transcendentals=0),
        name="receive_rows",
    )(got, ends)
    coarse_north = ring(coarse, "ny", -1)
    coarse_south = ring(coarse, "ny", 1)
    side_state, side_coef = pl.pallas_call(
        side_strips_kernel,
        out_shape=(frame(3, 2), frame(STEPS, 5, 2)),
        in_specs=[SMEM] + [VMEM] * 3 + [pl.BlockSpec(memory_space=pl.ANY)],
        out_specs=(VMEM, VMEM),
        scratch_shapes=[
            pltpu.VMEM((FTILE, FR + 8, LANES), F32),
            pltpu.VMEM((STEPS * FTILE, FR + 8, LANES), F32),
        ],
        compiler_params=limits(PREPARE_MIB),
        cost_estimate=pl.CostEstimate(flops=12_000_000, bytes_accessed=6_000_000, transcendentals=0),
        name="side_strips",
    )(shifts, ends, from_east, from_west, coarse)
    coarse_north, coarse_south, side_state = lax.optimization_barrier(
        (coarse_north, coarse_south, side_state)
    )
    north_flag = lax.axis_index("ny") < lax.axis_size("ny") - 1
    tall = jnp.concatenate(
        [coarse_south[:, 8:], coarse, jnp.where(north_flag, coarse_north[:, :8], 0.0)], axis=1
    )
    tall_east = ring(tall, "nx", -1)
    tall_west = ring(tall, "nx", 1)

    return pl.pallas_call(
        steps_kernel,
        out_shape=(sds((ROWS, COLS), F32),) * 3,
        in_specs=[SMEM] + [pl.BlockSpec(memory_space=pl.ANY)] * 5 + [VMEM] * 4,
        out_specs=(VMEM,) * 3,
        scratch_shapes=[
            pltpu.VMEM((3, FTILE, FR + 8, LANES), F32),
            pltpu.VMEM((3, FTILE, FR + 8, LANES), F32),
            pltpu.VMEM((STEPS, 5, FTILE - 2, FR, LANES), F32),
            pltpu.VMEM((STEPS, 5, 2, FR, LANES), F32),
            pltpu.VMEM((STEPS, 2 * LANES, FC), BF16),
            pltpu.SemaphoreType.DMA((9 + 3 * STEPS,)),
        ],
        compiler_params=limits(STEPS_MIB),
        cost_estimate=pl.CostEstimate(
            flops=400_000_000, bytes_accessed=23_000_000, transcendentals=0
        ),
        name="steps",
    )(shifts, mid_state, side_state, mid_coef, side_coef, cols, tall, tall_east, tall_west, edge)


def solution(mesh):
    in_specs = (
        P("ny", "nx"),
        P("ny", "nx"),
        P("ny", "nx"),
        P("ny", "nx"),
        P(None, "ny", "nx"),
        P(),
        P(None, ("ny", "nx"), None),
        P(None, ("ny", "nx")),
        P(None, ("ny", "nx")),
        P(None, "ny"),
        P(None, "nx", "ny"),
    )
    out_specs = (P("ny", "nx"), P("ny", "nx"), P("ny", "nx"))
    return jax.shard_map(local, mesh=mesh, in_specs=in_specs, out_specs=out_specs, check_vma=False)
```

```python
import functools

import jax
import jax.numpy as jnp
from jax import lax
from jax.experimental import pallas as pl
from jax.experimental.pallas import tpu as pltpu
from jax.sharding import PartitionSpec as P

RATIO = 9
STEPS = 4
CAP = 8
COARSE = 16
LANES = 128
ROWS, COLS = 144, 1152
FR, FC = 152, 1280
ROW0, COL0 = 4, 40
NHALO = 40
WIDTHS = (32, 24, 16, 8)
N_E, N_B, N_M = 0, 120, (152, 184, 208, 224)
N_ROWS, S_ROWS = 232, 64
CHUNK = 40
PREPARE_MIB, STEPS_MIB = 63, 63
META = 124
KTILE, FTILE = COLS // LANES, FC // LANES
E_PLACE = ((0, 0), (0, 40), (0, 80), (1, 0), (1, 64), (2, 0), (2, 32), (1, 32), (1, 88), (2, 16), (2, 40))
E_WIDTH = (40, 40, 40, 32, 24, 16, 8, 32, 24, 16, 8)

F32, BF16, I32 = jnp.float32, jnp.bfloat16, jnp.int32
VMEM = pl.BlockSpec(memory_space=pltpu.VMEM)
SMEM = pl.BlockSpec(memory_space=pltpu.SMEM)


def iota(shape, dim):
    return lax.broadcasted_iota(I32, shape, dim)


def left_over(shifts_ref, step, dim):
    total = jnp.int32(0)
    for later in range(STEPS):
        total += jnp.where(later > step, shifts_ref[dim, later], 0)
    return total


def halves(x):
    high = x.astype(BF16)
    return high, (x - high.astype(F32)).astype(BF16)


def dot(a, b, dims=((1,), (0,))):
    return lax.dot_general(a, b, (dims, ((), ())), preferred_element_type=F32)


def north_kernel(e_top, u_top, v_top, b_top, m_top, north_ref):
    for f, ref in enumerate((e_top, u_top, v_top)):
        north_ref[N_E + NHALO * f : N_E + NHALO * (f + 1), :] = ref[...]
    north_ref[N_B : N_B + WIDTHS[0], :] = b_top[...]
    for s in range(STEPS):
        north_ref[N_M[s] : N_M[s] + WIDTHS[s], :] = m_top[s, : WIDTHS[s], :].astype(F32)


def south_kernel(e_low, u_low, v_low, b_low, m_low, after_ref, south_ref):
    del after_ref
    for f, ref in enumerate((e_low, u_low, v_low, b_low)):
        south_ref[8 * f : 8 * f + 8, :] = ref[...]
    for s in range(STEPS):
        south_ref[32 + 8 * s : 40 + 8 * s, :] = m_low[s].astype(F32)


def pack_kernel(owner_ref, dest_ref, coarse_ref, vals_ref, panel_ref, after_ref, out_ref):
    del after_ref
    owners = out_ref.shape[0]
    count = dest_ref.shape[1]
    before = iota((count, count), 0) < iota((count, count), 1)
    unit = jnp.where(iota((count, count), 0) == iota((count, count), 1), 1.0, 0.0).astype(BF16)
    numbers = jnp.concatenate([dest_ref[...], coarse_ref[...] + 1], axis=0).astype(F32)
    upright = dot(unit, numbers.astype(BF16), ((1,), (1,)))
    lane = iota((count, LANES), 1)
    place_row = iota((owners * CAP, count), 0)
    meta = jnp.zeros((owners * CAP, LANES), F32)
    for s in range(STEPS):
        dest = dest_ref[s : s + 1, :]
        same = (upright[:, s : s + 1] == dest.astype(F32)) & before
        slot = jnp.sum(jnp.where(same, 1.0, 0.0), axis=0, keepdims=True).astype(I32)
        hits = jnp.where(place_row == dest * CAP + slot, 1.0, 0.0).astype(BF16)
        high, low = halves(vals_ref[s])
        target = jnp.where(lane == META + s, upright[:, STEPS + s : STEPS + s + 1], 0.0)
        out_ref[:, s * CAP : (s + 1) * CAP, :] = (dot(hits, high) + dot(hits, low)).reshape(
            owners, CAP, LANES
        )
        meta += dot(hits, target.astype(BF16))
    lane1 = iota((1, LANES), 1)
    first, second = [], []
    for s in range(STEPS):
        mine = owner_ref[0:1, s : s + 1] == lax.axis_index("nx")
        head = panel_ref[s, :, 0:LANES]
        tail = jnp.concatenate(
            [panel_ref[s, :, LANES:ROWS], jnp.zeros((1, 2 * LANES - ROWS), F32)], axis=1
        )
        first.append(jnp.where((lane1 < 120) & mine, head, 0.0))
        both = jnp.where(lane1 < 8, pltpu.roll(head, 8, 1), pltpu.roll(tail, 8, 1))
        second.append(jnp.where((lane1 < 24) & mine, both, 0.0))
    edges = jnp.concatenate(first + second, axis=0)
    out_ref[:, STEPS * CAP :, :] = meta.reshape(owners, CAP, LANES) + edges[None]


def receive_kernel(got_ref, after_ref, coarse_ref, edge_ref):
    del after_ref
    sources = got_ref.shape[0]
    meta = got_ref[:, STEPS * CAP :, :].reshape(sources * CAP, LANES)
    choose = jnp.where(iota((8, LANES), 1) == META + iota((8, LANES), 0), 1.0, 0.0)
    targets = dot(choose.astype(BF16), meta.astype(BF16), ((1,), (1,)))
    index = iota((COARSE, sources * CAP), 0)
    for s in range(STEPS):
        hits = jnp.where(index == targets[s : s + 1, :].astype(I32) - 1, 1.0, 0.0).astype(BF16)
        high, low = halves(got_ref[:, s * CAP : (s + 1) * CAP, :].reshape(sources * CAP, LANES))
        coarse_ref[s] = dot(hits, high) + dot(hits, low)
    row_block, col_groups = lax.axis_index("ny"), lax.axis_size("nx")
    for k in range(3):
        block = jnp.clip(row_block + k - 1, 0, lax.axis_size("ny") - 1)
        edge_ref[k] = jnp.sum(
            got_ref[pl.ds(block * col_groups, col_groups), STEPS * CAP :, :], axis=0
        )


def edge_flags():
    row_block, col_block = lax.axis_index("ny"), lax.axis_index("nx")
    south = jnp.where(row_block == 0, 0.0, 1.0).astype(F32)
    north = jnp.where(row_block == lax.axis_size("ny") - 1, 0.0, 1.0).astype(F32)
    west = jnp.where(col_block == 0, 0.0, 1.0).astype(F32)
    east = jnp.where(col_block == lax.axis_size("nx") - 1, 0.0, 1.0).astype(F32)
    return south, north, west, east


def fill_rows(tall_ref, own, south_ref, field, north_ref, north_at, width, flags):
    south, north = flags[0], flags[1]
    for k in range(tall_ref.shape[0]):
        lanes = slice(k * LANES, (k + 1) * LANES)
        tall_ref[k, 0:8, :] = south_ref[8 * field : 8 * field + 8, lanes] * south
        tall_ref[k, 8 : 8 + ROWS, :] = own(lanes)
        tall_ref[k, 8 + ROWS : 8 + ROWS + width, :] = (
            north_ref[north_at : north_at + width, lanes] * north
        )


def side_tiles(east_ref, west_ref, which, flags):
    tile, at = E_PLACE[which]
    right = east_ref[tile]
    if at:
        right = pltpu.roll(right, LANES - at, 1)
    left = pltpu.roll(west_ref[...], 120 - 8 * which, 1)
    return left * flags[2], right * flags[3]


def framed(ext, row_shift, col_shift, strips, write):
    lane = iota((FR, LANES), 1)
    turn = 128 - COL0 + col_shift
    amount = LANES - turn
    keep = lane < amount
    done, this = None, None
    for k in strips:
        if done != k:
            this = pltpu.roll(ext(k), amount, 1)
        following = pltpu.roll(ext(k + 1), amount, 1)
        write(k, jnp.where(keep, this, following))
        done, this = k + 1, following


def to_east(x, following, last_lane):
    return jnp.where(
        last_lane, pltpu.roll(following, LANES - 1, 1), pltpu.roll(x, LANES - 1, 1)
    )


def divide_18(n):
    return (n * 3641) >> 16


def frame_fields(
    shifts_ref, load, left_of, right_of, wet_ref, deep_ref,
    strips, state_to, coef_to, coef_strips, aside,
):
    def ext(which, tile_rows, row_shift):
        rows = pl.ds(row_shift + ROW0, FR)

        def tile(k):
            if k == 0:
                return left_of(which)
            if k == KTILE + 1:
                return right_of(which)
            return tile_rows(k - 1, rows)

        return tile

    row_all, col_all = left_over(shifts_ref, -1, 0), left_over(shifts_ref, -1, 1)
    for f in range(3):
        tiles = ext(f, load(f), row_all)
        aside(f, tiles)
        framed(tiles, row_all, col_all, coef_strips, functools.partial(state_to, f))
    wet_ref[:, FR:, :] = jnp.zeros_like(wet_ref[:, FR:, :])
    deep_ref[:, FR:, :] = jnp.zeros_like(deep_ref[:, FR:, :])
    last_lane = iota((8, LANES), 1) == LANES - 1
    row, lane = iota((FR, LANES), 0), iota((FR, LANES), 1)
    is_west = lax.axis_index("nx") == 0
    tile_rows = load(3)
    for s in range(STEPS):
        row_left, col_left = left_over(shifts_ref, s, 0), left_over(shifts_ref, s, 1)

        def write_depth(k, x, s=s):
            deep_ref[s * FTILE + k, 0:FR, :] = x

        tiles = ext(3 + s, tile_rows, row_left)
        aside(3 + s, tiles)
        framed(tiles, row_left, col_left, strips, write_depth)
    for s in range(STEPS):
        row_left, col_left = left_over(shifts_ref, s, 0), left_over(shifts_ref, s, 1)
        tiles = ext(7 + s, load(4 + s), row_left)
        aside(7 + s, tiles)
        nest_row = lax.axis_index("ny") * ROWS + row + row_left - ROW0
        in_nest = (nest_row >= 0) & (nest_row < ROWS * lax.axis_size("ny"))
        ghost = in_nest & (lane == COL0 - 1 - col_left) & is_west

        def write_wet(k, x, s=s, ghost=ghost):
            if k in coef_strips:
                coef_to(s, 4, k, slice(0, FR), x)
            wet_ref[k, 0:FR, :] = jnp.where(ghost, 1.0, x) if k == 0 else x

        framed(tiles, row_left, col_left, strips, write_wet)
        for k in coef_strips:
            east = min(k + 1, FTILE - 1)
            for at in range(0, FR, 8):
                tile, above = slice(at, at + 8), slice(at + 1, at + 9)
                wet, deep = wet_ref[k, tile, :], deep_ref[s * FTILE + k, tile, :]
                wet_e = to_east(wet, wet_ref[east, tile, :], last_lane)
                deep_e = to_east(deep, deep_ref[s * FTILE + east, tile, :], last_lane)
                wet = 0.0625 * wet
                open_x = wet * wet_e
                open_y = wet * wet_ref[k, above, :]
                coef_to(s, 0, k, tile, open_x)
                coef_to(s, 1, k, tile, open_x * (deep + deep_e))
                coef_to(s, 2, k, tile, open_y)
                coef_to(s, 3, k, tile, open_y * (deep + deep_ref[s * FTILE + k, above, :]))


def prepare_kernel(
    shifts_ref, e_ref, u_ref, v_ref, b_ref, m_ref, north_ref, south_ref,
    state_ref, coef_ref, cols_ref, ends_ref, east_ref, west_ref, tall_ref, wet_ref, deep_ref,
):
    flags = edge_flags()
    own_of = [lambda lanes, ref=ref: ref[:, lanes] for ref in (e_ref, u_ref, v_ref, b_ref)]
    own_of += [lambda lanes, s=s: m_ref[s, :, lanes].astype(F32) for s in range(STEPS)]
    starts = (N_E, N_E + NHALO, N_E + 2 * NHALO, N_B, *N_M)
    widths = (NHALO,) * 3 + (WIDTHS[0],) + WIDTHS
    lane = iota((FR, LANES), 1)
    tall_ref[...] = jnp.zeros_like(tall_ref)
    east_ref[...] = jnp.zeros_like(east_ref)
    west_ref[...] = jnp.zeros_like(west_ref)

    def load(field):
        fill_rows(
            tall_ref, own_of[field], south_ref, field, north_ref, starts[field], widths[field], flags
        )
        for place, k in enumerate((0, 1, KTILE - 1)):
            ends_ref[field, place] = tall_ref[k]
        return lambda k, rows: tall_ref[k, rows, :]

    def aside(which, tiles):
        (tile, at), width = E_PLACE[which], E_WIDTH[which]
        moved = pltpu.roll(tiles(1), at, 1) if at else tiles(1)
        east_ref[tile] = jnp.where((lane >= at) & (lane < at + width), moved, east_ref[tile])
        at = 8 * which
        moved = pltpu.roll(tiles(KTILE), at + 8, 1)
        west_ref[...] = jnp.where((lane >= at) & (lane < at + 8), moved, west_ref[...])

    def none(which):
        return jnp.zeros((FR, LANES), F32)

    def state_to(f, k, x):
        state_ref[f, k - 1] = x

    def coef_to(s, c, k, rows, x):
        coef_ref[s, c, k - 1, rows, :] = x

    frame_fields(
        shifts_ref, load, none, none, wet_ref, deep_ref,
        range(1, FTILE), state_to, coef_to, range(1, FTILE - 1), aside,
    )
    for s in range(STEPS):
        col = iota((1, FC), 1) + left_over(shifts_ref, s, 1) - COL0
        inside = jnp.where(col < 0, col + COLS, jnp.where(col >= COLS, col - COLS, col))
        numerator = 2 * inside + 1 - RATIO
        lower = jnp.clip(divide_18(numerator + 18) - 1, 0, LANES - 2)
        weight = jnp.clip(numerator - 18 * lower, 0, 18)
        first = lower + jnp.where((col < 0) | (col >= COLS), LANES, 0)
        for part in range(2):
            place = iota((LANES, FC), 0) + part * LANES
            cols_ref[s, part * LANES : (part + 1) * LANES, :] = jnp.where(
                place == first, 18 - weight, jnp.where(place == first + 1, weight, 0)
            ).astype(F32).astype(BF16)


def side_strips_kernel(
    shifts_ref, ends_ref, east_ref, west_ref, after_ref, state_ref, coef_ref, wet_ref, deep_ref
):
    del after_ref
    flags = edge_flags()

    def load(field):
        return lambda k, rows: ends_ref[field, min(k, 2), rows, :]

    def state_to(f, k, x):
        state_ref[f, 1 if k else 0] = x

    def coef_to(s, c, k, rows, x):
        coef_ref[s, c, 1 if k else 0, rows, :] = x

    frame_fields(
        shifts_ref,
        load,
        lambda which: side_tiles(east_ref, west_ref, which, flags)[0],
        lambda which: side_tiles(east_ref, west_ref, which, flags)[1],
        wet_ref,
        deep_ref,
        (0, 1, FTILE - 1),
        state_to,
        coef_to,
        (0, FTILE - 1),
        lambda which, tiles: None,
    )


def one_step(
    s, shifts_ref, mid_ref, side_ref, cols_ref, own_ref, east_ref, west_ref, edge_ref, cur, new
):
    row_left, col_left = left_over(shifts_ref, s, 0), left_over(shifts_ref, s, 1)
    is_west = lax.axis_index("nx") == 0
    east = jnp.where(lax.axis_index("nx") == lax.axis_size("nx") - 1, 0.0, 1.0).astype(F32)

    i = iota((FR, 1), 0) + row_left - ROW0
    block = jnp.where(i < 0, 0, jnp.where(i >= ROWS, 2, 1))
    inside = i - (block - 1) * ROWS
    numerator = 2 * inside + 1 - RATIO
    lower = jnp.clip(divide_18(numerator + 18) - 1, 0, COARSE - 2)
    weight = jnp.clip(numerator - 18 * lower, 0, 18)
    first = lower + 16 * block - 8
    place = iota((FR, 32), 1)
    rows = jnp.where(place == first, 18 - weight, jnp.where(place == first + 1, weight, 0))
    rows = rows.astype(F32).astype(BF16)
    side = jnp.where(iota((32, LANES), 1) < 64, east_ref[s] * east, west_ref[s])
    parts = []
    for x in (own_ref[s], side):
        high, low = halves(x)
        parts.append(dot(rows, high) + dot(rows, low))
    section = jnp.concatenate(parts, axis=1) * (1.0 / 324.0)
    high, low = halves(section)
    for k in range(0, FTILE, 2):
        lanes = slice(k * LANES, (k + 2) * LANES)
        rise = dot(high, cols_ref[s, :, lanes]) + dot(low, cols_ref[s, :, lanes])
        cur[0, k, 0:FR, :] += rise[:, :LANES]
        cur[0, k + 1, 0:FR, :] += rise[:, LANES:]

    half = jnp.where(inside >= 120, 1, 0)
    pick = jnp.where(iota((FR, 24), 1) == 8 * block + 4 * half + s, 1.0, 0.0).astype(BF16)
    high, low = halves(edge_ref[...].reshape(24, LANES))
    line = dot(pick, high) + dot(pick, low)
    lane = iota((FR, LANES), 1)
    edge = jnp.sum(jnp.where(lane == inside - 120 * half, line, 0.0), axis=1, keepdims=True)
    ghost = (lane == COL0 - 1 - col_left) & is_west

    cur[0, 0, 0:FR, :] = jnp.where(ghost, edge, cur[0, 0, 0:FR, :])
    cur[1, 0, 0:FR, :] = jnp.where(ghost, 0.0, cur[1, 0, 0:FR, :])
    cur[2, 0, 0:FR, :] = jnp.where(ghost, 0.0, cur[2, 0, 0:FR, :])
    def cat(f, rows):
        return jnp.concatenate([cur[f, k, rows, :] for k in range(FTILE)], axis=1)

    def coefficient(c, rows):
        tiles = [mid_ref[s, c, k, rows, :] for k in range(FTILE - 2)]
        ends = [side_ref[s, c, k, rows, :] for k in range(2)]
        return jnp.concatenate([ends[0], *tiles, ends[1]], axis=1)

    first_row = iota((8, FC), 0) == 0
    south = [jnp.zeros((8, FC), F32)] * 3
    for at in range(0, FR, 8):
        tile, above = slice(at, at + 8), slice(at + 1, at + 9)
        E, U, V = (cat(f, tile) for f in range(3))
        Ee, Ue, Ve = (pltpu.roll(x, FC - 1, 1) for x in (E, U, V))
        bx, cx, by, cy, inner = (coefficient(c, tile) for c in range(5))
        across = (
            bx * (2.0 * (U + Ue) - (Ee - E)),
            cx * (E + Ee) - bx * (Ue - U),
            bx * (V - Ve),
        )
        out = [x - (a - pltpu.roll(a, 1, 1)) for x, a in zip((E, U, V), across)]
        En, Un, Vn = (cat(f, above) for f in range(3))
        along = (
            by * (2.0 * (V + Vn) - (En - E)),
            by * (U - Un),
            cy * (E + En) - by * (Vn - V),
        )
        for f in range(3):
            lifted = pltpu.roll(along[f], 1, 0)
            out[f] = out[f] - (along[f] - jnp.where(first_row, south[f], lifted))
            south[f] = lifted
        out = (out[0], inner * out[1], inner * out[2])
        for f in range(3):
            for k in range(FTILE):
                new[f, k, tile, :] = out[f][:, k * LANES : (k + 1) * LANES]


def steps_kernel(
    shifts_ref, mid_state, side_state, mid_hbm, side_hbm, cols_hbm, own_ref, east_ref, west_ref,
    edge_ref, e_out, u_out, v_out, even, odd, mid_ref, side_ref, cols_ref, sems,
):
    copies = []
    for f in range(3):
        copies.append(
            pltpu.make_async_copy(
                mid_state.at[f], even.at[f, 1 : FTILE - 1, 0:FR, :], sems.at[f]
            )
        )
        for end, k in enumerate((0, FTILE - 1)):
            copies.append(
                pltpu.make_async_copy(
                    side_state.at[f, end], even.at[f, k, 0:FR, :], sems.at[3 + 2 * f + end]
                )
            )
    per_step = []
    for s in range(STEPS):
        pairs = ((cols_hbm, cols_ref), (mid_hbm, mid_ref), (side_hbm, side_ref))
        per_step.append(
            [
                pltpu.make_async_copy(a.at[s], b.at[s], sems.at[9 + 3 * s + i])
                for i, (a, b) in enumerate(pairs)
            ]
        )
    for copy in copies:
        copy.start()
    for copy in per_step[0]:
        copy.start()
    for f in range(3):
        for k in range(FTILE):
            even[f, k, FR:, :] = jnp.zeros((8, LANES), F32)
            odd[f, k, FR:, :] = jnp.zeros((8, LANES), F32)
    for copy in copies:
        copy.wait()
    cur, new = even, odd
    for s in range(STEPS):
        for copy in per_step[s]:
            copy.wait()
        if s + 1 < STEPS:
            for copy in per_step[s + 1]:
                copy.start()
        one_step(
            s, shifts_ref, mid_ref, side_ref, cols_ref, own_ref, east_ref, west_ref, edge_ref,
            cur, new,
        )
        cur, new = new, cur
    keep = iota((ROWS, LANES), 1) < LANES - COL0
    rows = slice(ROW0, ROW0 + ROWS)
    for f, ref in enumerate((e_out, u_out, v_out)):
        this = pltpu.roll(cur[f, 0, rows, :], LANES - COL0, 1)
        for k in range(KTILE):
            following = pltpu.roll(cur[f, k + 1, rows, :], LANES - COL0, 1)
            ref[:, k * LANES : (k + 1) * LANES] = jnp.where(keep, this, following)
            this = following


def ring(value, axis, by):
    count = lax.axis_size(axis)
    return lax.ppermute(value, axis, [(i, (i + by) % count) for i in range(count)])


def limits(mib, **more):
    return pltpu.CompilerParams(vmem_limit_bytes=mib * 1024 * 1024, **more)


def local(
    elevation, flux_x, flux_y, depth, wet_mask, shifts, parent_vals, row_dest, row_coarse,
    edge_owner, edge_panels,
):
    shifts = shifts.T
    owners = lax.axis_size("ny") * lax.axis_size("nx")
    sds = jax.ShapeDtypeStruct
    top = lambda rows: pl.BlockSpec((rows, COLS), lambda g: (0, 0))
    low = pl.BlockSpec((8, COLS), lambda g: (ROWS // 8 - 1, 0))
    fields = (elevation, flux_x, flux_y, depth, wet_mask)
    north_message = pl.pallas_call(
        north_kernel,
        out_shape=sds((N_ROWS, COLS), F32),
        grid=(1,),
        in_specs=[top(NHALO)] * 3
        + [top(WIDTHS[0]), pl.BlockSpec((STEPS, WIDTHS[0], COLS), lambda g: (0, 0, 0))],
        out_specs=top(N_ROWS),
        compiler_params=limits(63),
        cost_estimate=pl.CostEstimate(flops=300_000, bytes_accessed=2_200_000, transcendentals=0),
        name="north_message",
    )(*fields)
    south_message = pl.pallas_call(
        south_kernel,
        out_shape=sds((S_ROWS, COLS), F32),
        grid=(1,),
        in_specs=[low] * 4
        + [pl.BlockSpec((STEPS, 8, COLS), lambda g: (0, ROWS // 8 - 1, 0))]
        + [pl.BlockSpec(memory_space=pl.ANY)],
        out_specs=top(S_ROWS),
        compiler_params=limits(63),
        cost_estimate=pl.CostEstimate(flops=80_000, bytes_accessed=600_000, transcendentals=0),
        name="south_message",
    )(*fields, north_message)
    from_north = ring(north_message, "ny", -1)
    from_south = ring(south_message, "ny", 1)

    send = pl.pallas_call(
        pack_kernel,
        out_shape=sds((owners, CHUNK, LANES), F32),
        in_specs=[VMEM] * 5 + [pl.BlockSpec(memory_space=pl.ANY)],
        out_specs=VMEM,
        compiler_params=limits(63),
        cost_estimate=pl.CostEstimate(flops=800_000_000, bytes_accessed=3_200_000, transcendentals=0),
        name="pack_rows",
    )(edge_owner.reshape(1, STEPS), row_dest, row_coarse, parent_vals, edge_panels, south_message)
    send, from_south, from_north = lax.optimization_barrier((send, from_south, from_north))
    got = lax.all_to_all(send, ("ny", "nx"), split_axis=0, concat_axis=0, tiled=True)

    frame = lambda *lead: sds((*lead, FR, LANES), F32)
    tall_rows = 16 + ROWS + NHALO
    mid_state, mid_coef, cols, ends, east_side, west_side = pl.pallas_call(
        prepare_kernel,
        out_shape=(
            frame(3, FTILE - 2),
            frame(STEPS, 5, FTILE - 2),
            sds((STEPS, 2 * LANES, FC), BF16),
            sds((4 + STEPS, 3, tall_rows, LANES), F32),
            frame(3),
            frame(),
        ),
        in_specs=[SMEM] + [VMEM] * 7,
        out_specs=(VMEM,) * 6,
        scratch_shapes=[
            pltpu.VMEM((KTILE, tall_rows, LANES), F32),
            pltpu.VMEM((FTILE, FR + 8, LANES), F32),
            pltpu.VMEM((STEPS * FTILE, FR + 8, LANES), F32),
        ],
        compiler_params=limits(PREPARE_MIB),
        cost_estimate=pl.CostEstimate(
            flops=60_000_000, bytes_accessed=27_000_000, transcendentals=0
        ),
        name="prepare",
    )(shifts, *fields, from_north, from_south)
    from_east = ring(east_side, "nx", -1)
    from_west = ring(west_side, "nx", 1)

    coarse, edge = pl.pallas_call(
        receive_kernel,
        out_shape=(sds((STEPS, COARSE, LANES), F32), sds((3, CAP, LANES), F32)),
        in_specs=[VMEM, pl.BlockSpec(memory_space=pl.ANY)],
        out_specs=(VMEM, VMEM),
        compiler_params=limits(63),
        cost_estimate=pl.CostEstimate(flops=300_000_000, bytes_accessed=2_700_000, transcendentals=0),
        name="receive_rows",
    )(got, ends)
    coarse_north = ring(coarse, "ny", -1)
    coarse_south = ring(coarse, "ny", 1)
    side_state, side_coef = pl.pallas_call(
        side_strips_kernel,
        out_shape=(frame(3, 2), frame(STEPS, 5, 2)),
        in_specs=[SMEM] + [VMEM] * 3 + [pl.BlockSpec(memory_space=pl.ANY)],
        out_specs=(VMEM, VMEM),
        scratch_shapes=[
            pltpu.VMEM((FTILE, FR + 8, LANES), F32),
            pltpu.VMEM((STEPS * FTILE, FR + 8, LANES), F32),
        ],
        compiler_params=limits(PREPARE_MIB),
        cost_estimate=pl.CostEstimate(flops=12_000_000, bytes_accessed=6_000_000, transcendentals=0),
        name="side_strips",
    )(shifts, ends, from_east, from_west, coarse)
    coarse_north, coarse_south, side_state = lax.optimization_barrier(
        (coarse_north, coarse_south, side_state)
    )
    north_flag = lax.axis_index("ny") < lax.axis_size("ny") - 1
    tall = jnp.concatenate(
        [coarse_south[:, 8:], coarse, jnp.where(north_flag, coarse_north[:, :8], 0.0)], axis=1
    )
    tall_east = ring(tall, "nx", -1)
    tall_west = ring(tall, "nx", 1)

    return pl.pallas_call(
        steps_kernel,
        out_shape=(sds((ROWS, COLS), F32),) * 3,
        in_specs=[SMEM] + [pl.BlockSpec(memory_space=pl.ANY)] * 5 + [VMEM] * 4,
        out_specs=(VMEM,) * 3,
        scratch_shapes=[
            pltpu.VMEM((3, FTILE, FR + 8, LANES), F32),
            pltpu.VMEM((3, FTILE, FR + 8, LANES), F32),
            pltpu.VMEM((STEPS, 5, FTILE - 2, FR, LANES), F32),
            pltpu.VMEM((STEPS, 5, 2, FR, LANES), F32),
            pltpu.VMEM((STEPS, 2 * LANES, FC), BF16),
            pltpu.SemaphoreType.DMA((9 + 3 * STEPS,)),
        ],
        compiler_params=limits(STEPS_MIB),
        cost_estimate=pl.CostEstimate(
            flops=400_000_000, bytes_accessed=23_000_000, transcendentals=0
        ),
        name="steps",
    )(shifts, mid_state, side_state, mid_coef, side_coef, cols, tall, tall_east, tall_west, edge)


def solution(mesh):
    in_specs = (
        P("ny", "nx"),
        P("ny", "nx"),
        P("ny", "nx"),
        P("ny", "nx"),
        P(None, "ny", "nx"),
        P(),
        P(None, ("ny", "nx"), None),
        P(None, ("ny", "nx")),
        P(None, ("ny", "nx")),
        P(None, "ny"),
        P(None, "nx", "ny"),
    )
    out_specs = (P("ny", "nx"), P("ny", "nx"), P("ny", "nx"))
    return jax.shard_map(local, mesh=mesh, in_specs=in_specs, out_specs=out_specs, check_vma=False)
```
